256 devices in a mesh: band: 4 (over y), gx: 16 (over z, core), gy: 4 (over x).
Axes of the slice: x: 4, y: 4, z: 8, core: 2. Of those that a mesh axis runs over, the one named last changes fastest.
Arguments:
- ensemble: bfloat16 [4, 16, 1408, 2560], P('band', None, ('gx', 'gy')), may hold values from -6 to 6
- spectral: bfloat16 [4, 2, 1024, 16, 256], P('band', None, 'gx', 'gy'), may hold values from -6 to 6
- band_cut: int32 [4], replicated, may hold values from 1 to 327680, as said below
Outputs:
- increment: float32 [1408, 2560], P(('gx', 'gy'), 'band')
The draws below stay inside these ranges and needn't reach their ends.
Inputs may be any that keep to these rules, and one draw needn't show every extreme that they name: band_cut rises strictly from band to band, and the last band's value exceeds (j - 512)^2 + ky^2 for every wavenumber pair of the control fields.
All inputs are finite; a program needn't handle non-finite values.
Results may differ from the reference program's by a relative error of at most 0.0044.
Values may be sent and summed in bfloat16 or wider, within the bound.
No kernel may reach another device: no remote copies, remote signals or barrier semaphores. Data moves between devices by JAX's collectives and lax.ppermute only.
A program may use at most 64 MiB of HBM per device.

```python
import math
import jax
import jax.numpy as jnp
from jax import lax

NX = 2560
NY = 1408
KX = 1024
KY = 256
M = 16
B = 4


def draw_band_cut(key, part):
    key = jax.random.fold_in(key, 7)
    levels = jnp.arange(B, dtype=jnp.int32)
    base_value = ((levels + 1) * KX // (2 * B)) ** 2
    low_value = base_value // 2
    random_bits = jax.random.randint(key, (B,), 0, 1 << 20)
    chosen = low_value + jnp.mod(random_bits, base_value - low_value + 1)
    largest = (KX // 2) ** 2 + KY ** 2
    return jnp.where(levels == B - 1, largest, chosen).astype(jnp.int32)


def block_scale(key, extent, shards, least, high):
    loudness = 1.0
    for position, shards_of in shards:
        heights = jax.random.uniform(jax.random.fold_in(jax.random.fold_in(key, 6), position), (shards_of,), jnp.float32, least / len(shards), high / len(shards))
        loudness = loudness * jnp.repeat(jnp.exp(heights), extent[position] // shards_of).reshape((-1,) + (1,) * (len(extent) - 1 - position))
    return loudness


def gaussian(stream_key, shape, scale, most, split=(), held_as=jnp.bfloat16):
    entries = jax.random.normal(stream_key, shape, jnp.float32) * scale
    if len(split) > 0:
        entries = block_scale(stream_key, shape, split, -0.22, 0.18) * entries
    return jnp.clip(entries, min=-most, max=most).astype(held_as)


def setup_inputs(seed: int = 0) -> dict:
    splits = jax.random.split(jax.random.key(seed), 4)
    return {
        "ensemble": gaussian(splits[0], (B, M, NY, NX), 1.0, 6.0, ((0, 4), (2, 64))),
        "spectral": gaussian(splits[1], (B, 2, KX, M, KY), 1.0, 6.0, ((0, 4), (2, 16), (3, 4))),
        "band_cut": draw_band_cut(jax.random.fold_in(splits[3], 71), 0),
    }


def table_along_y():
    wave_y = jnp.arange(KY, dtype=jnp.int32)[:, None]
    positions = jnp.arange(NY, dtype=jnp.int32)[None, :]
    phase_angle = jnp.mod(wave_y * positions, NY).astype(jnp.float32) * (2.0 * math.pi / NY)
    return jnp.concatenate([jnp.cos(phase_angle), jnp.sin(phase_angle)], axis=1).astype(jnp.bfloat16)

def table_along_x():
    wave_x = (jnp.arange(KX, dtype=jnp.int32) - KX // 2)[:, None]
    positions = jnp.arange(NX, dtype=jnp.int32)[None, :]
    phase_angle = jnp.mod(wave_x * positions, NX).astype(jnp.float32) * (2.0 * math.pi / NX)
    return jnp.concatenate([jnp.cos(phase_angle), -jnp.sin(phase_angle)], axis=0).astype(jnp.bfloat16)

def wave_mask(first_row, wave_rows, band_limit):
    wave_x = first_row + jnp.arange(wave_rows, dtype=jnp.int32) - KX // 2
    wave_y = jnp.arange(KY, dtype=jnp.int32)
    return wave_x[:, None] ** 2 + wave_y[None, :] ** 2 < band_limit

def along_y(masked, table_y):
    product = jnp.dot(masked.reshape(-1, KY), table_y, preferred_element_type=jnp.float32)
    product = product.reshape(2, -1, 2, NY)
    real_part = product[0, :, 0] - product[1, :, 1]
    imag_part = product[0, :, 1] + product[1, :, 0]
    return jnp.stack([real_part, imag_part]).astype(jnp.bfloat16)

def reference(ensemble, spectral, band_cut):
    table_y = table_along_y()
    table_x = table_along_x()

    def one_band(operands):
        band_fields, band_coeffs, band_limit = operands
        inside = wave_mask(0, KX, band_limit)
        norm_scale = lax.rsqrt(jnp.sum(inside.astype(jnp.int32)).astype(jnp.float32))
        weights = inside.astype(jnp.bfloat16)

        def add_member(member, running):
            member_coeffs = lax.dynamic_index_in_dim(band_coeffs, member, 2, keepdims=False)
            spectra = along_y(member_coeffs * weights[None], table_y)
            alpha_field = jnp.dot(spectra.reshape(2 * KX, NY).T, table_x, preferred_element_type=jnp.float32) * norm_scale
            member_field = lax.dynamic_index_in_dim(band_fields, member, 0, keepdims=False).astype(jnp.float32)
            return running + alpha_field * member_field
        return lax.fori_loop(0, M, add_member, jnp.zeros((NY, NX), jnp.float32))
    partial_sums = lax.map(one_band, (ensemble, spectral, band_cut))
    return lax.optimization_barrier(jnp.sum(partial_sums, axis=0)) * (1.0 / math.sqrt(M * B))
```

```python
import functools
import math

import jax
import jax.numpy as jnp
import ml_dtypes
import numpy as np
from jax import lax
from jax.experimental import pallas as pl
from jax.experimental.pallas import tpu as pltpu
from jax.sharding import PartitionSpec as P

NX = 2560
NY = 1408
KX = 1024
KY = 256
M = 16
BANDS = 4
GX = 16
GY = 4
DESTS = GX * GY
ROWS = NY // DESTS
PAD = 24
WAVES = KX // GX
HALF = WAVES // 2
MEMBERS = M // GY
CHUNK = NX // BANDS
SCRATCH = 16 * 1024 * 1024
OWN_FLOPS = 10 ** 10
ROWS_FLOPS = 2 * 10 ** 10


def low(array):
    return np.asarray(array, dtype=np.float64).astype(ml_dtypes.bfloat16)


def trig(wave, position, period):
    angle = np.mod(np.multiply.outer(wave, position), period) * (2.0 * math.pi / period)
    return np.cos(angle), np.sin(angle)


def first_wave(block):
    return WAVES * (block - GX // 2) if block >= GX // 2 else WAVES * (GX // 2 - 1 - block) + HALF


@functools.lru_cache(None)
def fold_tables():
    fold = np.zeros((2, 2, MEMBERS, HALF, (WAVES + HALF) * MEMBERS))
    for member in range(MEMBERS):
        for pair in range(HALF):
            own = MEMBERS * pair + member
            for part, sign in ((0, 1.0), (1, -1.0)):
                fold[0, part, member, pair, own] = 1.0
                if pair > 0:
                    fold[0, part, member, pair, MEMBERS * (WAVES + HALF - pair) + member] = sign
                fold[1, part, member, pair, MEMBERS * WAVES + own] = 1.0
                fold[1, part, member, pair, MEMBERS * (HALF - pair) + member] = sign
    return low(fold.reshape(2, 2 * MEMBERS * HALF, (WAVES + HALF) * MEMBERS))


@functools.lru_cache(None)
def row_tables():
    cosine, sine = trig(np.arange(NY), np.arange(KY), NY)
    table = np.zeros((DESTS, PAD, 2 * KY + 128))
    table[:, :ROWS, :KY] = cosine.reshape(DESTS, ROWS, KY)
    table[:, :ROWS, KY : 2 * KY] = sine.reshape(DESTS, ROWS, KY)
    table[np.arange(DESTS), ROWS, 2 * KY + np.arange(DESTS)] = 1.0
    coarse = np.zeros((128, 2 * KY))
    coarse[:DESTS] = np.concatenate(trig(np.arange(DESTS) * ROWS, np.arange(KY), NY), axis=1)
    fine = np.stack(trig(np.arange(32), np.arange(KY), NY)).astype(np.float32)
    return low(table.reshape(DESTS * PAD, -1)), low(coarse), fine


@functools.lru_cache(None)
def column_tables():
    waves = np.concatenate([first_wave(block) + np.arange(HALF) for block in range(GX)])
    cosine, sine = trig(waves, np.arange(NX), NX)
    extra = np.repeat(KX // 2 - WAVES * np.arange(GX // 2), GY)
    extra_cosine, extra_sine = trig(extra, np.arange(NX), NX)
    return low(np.concatenate([cosine, -sine, extra_cosine, extra_sine, np.zeros((64, NX))]))


@functools.lru_cache(None)
def order_tables():
    lanes = np.arange(512)
    lane_order = np.zeros((512, 512))
    block, member, pair = lanes // 128, lanes // 32 % 4, lanes % 32
    lane_order[lanes, member * 128 + block * 32 + pair] = 1.0
    row_order = np.zeros((ROWS, GY, MEMBERS, MEMBERS, GY, PAD))
    pick = np.zeros((ROWS, GY, MEMBERS, 2, MEMBERS, 32))
    same = np.zeros((ROWS, GY, MEMBERS, 128))
    for row in range(ROWS):
        for column in range(GY):
            for member in range(MEMBERS):
                row_order[row, column, member, member, column, row] = 1.0
                pick[row, column, member, :, member, row] = 1.0
                same[row, column, member, column:64:GY] = 1.0
    gather = np.zeros((128, DESTS // 2, PAD))
    lane_part = np.zeros((128, 256))
    for slot in range(64):
        gather[slot, slot % 32, ROWS] = 1.0
        lane_part[slot, slot // 32 * 128 : slot // 32 * 128 + 128] = 1.0
    return (
        low(lane_order),
        low(row_order.reshape(ROWS * M, MEMBERS * GY * PAD)),
        low(pick.reshape(ROWS * M, 256)),
        same.reshape(ROWS * M, 128).astype(np.float32),
        low(gather.reshape(128, DESTS // 2 * PAD)),
        lane_part.astype(np.float32),
    )


def nn(a, b):
    return jnp.dot(a, b, preferred_element_type=jnp.float32)


def nt(a, b):
    return lax.dot_general(a, b, (((1,), (1,)), ((), ())), preferred_element_type=jnp.float32)


def place(block, rows):
    negative = (block < GX // 2).astype(jnp.int32)
    return negative, jnp.where(negative == 1, WAVES * (GX // 2 - 1 - block), WAVES * (block - GX // 2))


def pair_mask(base, negative, cut):
    shape = (2 * MEMBERS * HALF, KY)
    wave = base + HALF * negative + (lax.broadcasted_iota(jnp.int32, shape, 0) & (HALF - 1))
    wave_y = lax.broadcasted_iota(jnp.int32, shape, 1)
    return wave * wave + wave_y * wave_y < cut


def own_kernel(cut_ref, own_ref, fold_ref, coarse_ref, fine_ref, folded_ref, extra_ref, scale_ref):
    block = lax.axis_index("gx")
    cut = cut_ref[lax.axis_index("band")]
    negative, base = place(block, WAVES)
    fold = fold_ref[negative, :, : WAVES * MEMBERS]
    inside = pair_mask(base, negative, cut)
    for part in range(2):
        folded_ref[part] = jnp.where(inside, nn(fold, own_ref[part]), 0.0)

    wave_y = lax.broadcasted_iota(jnp.int32, (MEMBERS, KY), 1)
    last = base + WAVES
    edge = last * last + wave_y * wave_y < cut
    edge_real = jnp.where(edge, own_ref[0, :16].astype(jnp.float32)[:MEMBERS], 0.0)
    edge_imag = jnp.where(edge, own_ref[1, :16].astype(jnp.float32)[:MEMBERS], 0.0)
    cosine, sine = fine_ref[0], fine_ref[1]
    even = jnp.concatenate(
        [edge_real[m : m + 1] * cosine - edge_imag[m : m + 1] * sine for m in range(MEMBERS)], axis=0
    )
    odd = jnp.concatenate(
        [edge_real[m : m + 1] * sine + edge_imag[m : m + 1] * cosine for m in range(MEMBERS)], axis=0
    )
    turned = jnp.concatenate(
        [jnp.concatenate([even, -odd], axis=1), jnp.concatenate([odd, even], axis=1)], axis=0
    ).astype(jnp.bfloat16)
    extra_ref[...] = nt(turned, coarse_ref[...]).astype(jnp.bfloat16)

    shape = (KX, KY)
    wave_x = lax.broadcasted_iota(jnp.int32, shape, 0) - KX // 2
    wave_y = lax.broadcasted_iota(jnp.int32, shape, 1)
    inside = (wave_x * wave_x + wave_y * wave_y < cut).astype(jnp.float32)
    count = jnp.sum(jnp.sum(inside.reshape(KX // 8, 8, KY), axis=0))
    scale_ref[...] = lax.rsqrt(jnp.full((8, 128), count)) * (1.0 / math.sqrt(M * BANDS))


def rows_kernel(cut_ref, folded_ref, extra_ref, mirror_ref, fold_ref, table_ref, out_ref):
    cut = cut_ref[lax.axis_index("band")]
    negative, base = place(lax.axis_index("gx"), WAVES)
    fold = fold_ref[negative, :, WAVES * MEMBERS :]
    inside = pair_mask(base, negative, cut)
    real = folded_ref[0] + jnp.where(inside, nn(fold, mirror_ref[0]), 0.0)
    imag = folded_ref[1] + jnp.where(inside, nn(fold, mirror_ref[1]), 0.0)
    half = MEMBERS * HALF
    with_cosine = jnp.concatenate([real[:half], imag[half:]], axis=0)
    with_sine = jnp.concatenate([-imag[:half], real[half:]], axis=0)
    weights = jnp.concatenate([with_cosine, with_sine], axis=1).astype(jnp.bfloat16)
    weights = jnp.concatenate([weights, extra_ref[...]], axis=1)
    for part in range(4):
        rows = pl.ds(part * 384, 384)
        out_ref[rows, :] = nt(table_ref[rows, :], weights).astype(jnp.bfloat16)


def field_kernel(
    scale_ref, got_ref, ensemble_ref, table_ref, lane_ref, row_ref, pick_ref, same_ref, gather_ref, part_ref, *rest
):
    outs, joined = rest[:BANDS], rest[BANDS]
    span = GY * PAD
    groups = []
    for part in range(2):
        for high in range(4):
            groups.append(
                jnp.concatenate(
                    [
                        got_ref[(4 * high + least) * span : (4 * high + least + 1) * span, part * 128 : part * 128 + 128]
                        for least in range(4)
                    ],
                    axis=1,
                )
            )
    ordered = nn(jnp.concatenate(groups, axis=0), lane_ref[...]).astype(jnp.bfloat16)
    members = [
        jnp.concatenate(
            [ordered[group * span : (group + 1) * span, m * 128 : m * 128 + 128] for group in range(8)], axis=1
        )
        for m in range(MEMBERS)
    ]
    joined[:, : 2 * KX // 2] = nn(row_ref[...], jnp.concatenate(members, axis=0)).astype(jnp.bfloat16)
    edge = nn(gather_ref[...], got_ref[: DESTS // 2 * PAD, :]) * part_ref[...]
    joined[:, KX:] = (nt(pick_ref[...], edge.astype(jnp.bfloat16)) * same_ref[...]).astype(jnp.bfloat16)
    scale = scale_ref[:1, :1]
    band = lax.axis_index("band")
    for step in range(BANDS):
        start = pl.multiple_of(lax.rem(band + step, BANDS) * CHUNK, CHUNK)
        columns = pl.ds(start, CHUNK)
        alpha = nn(joined[...], table_ref[:, columns]).reshape(ROWS, M, CHUNK)
        weighted = alpha * ensemble_ref[:, :, columns].astype(jnp.float32)
        outs[step][...] = jnp.sum(weighted, axis=1) * scale


def whole(count):
    return [pl.BlockSpec(memory_space=pltpu.VMEM) for _ in range(count)]


def body(ensemble, spectral, band_cut):
    own = spectral[0].reshape(2, WAVES * MEMBERS, KY)
    mirror = lax.ppermute(own[:, HALF * MEMBERS :], "gx", [(i, GX - 1 - i) for i in range(GX)])
    table_y, coarse, fine = row_tables()
    smem = pl.BlockSpec(memory_space=pltpu.SMEM)
    folded, extra, scale = pl.pallas_call(
        own_kernel,
        out_shape=[
            jax.ShapeDtypeStruct((2, 256, KY), jnp.float32),
            jax.ShapeDtypeStruct((256, 128), jnp.bfloat16),
            jax.ShapeDtypeStruct((8, 128), jnp.float32),
        ],
        in_specs=[smem] + whole(4),
        out_specs=whole(3),
        compiler_params=pltpu.CompilerParams(vmem_limit_bytes=SCRATCH),
        cost_estimate=pl.CostEstimate(flops=OWN_FLOPS, bytes_accessed=1 << 20, transcendentals=0),
        name="own_kernel",
    )(band_cut, own, fold_tables(), coarse, fine)
    rows = pl.pallas_call(
        rows_kernel,
        out_shape=jax.ShapeDtypeStruct((DESTS * PAD, 256), jnp.bfloat16),
        in_specs=[smem] + whole(5),
        out_specs=pl.BlockSpec(memory_space=pltpu.VMEM),
        compiler_params=pltpu.CompilerParams(vmem_limit_bytes=SCRATCH),
        cost_estimate=pl.CostEstimate(flops=ROWS_FLOPS, bytes_accessed=4 << 20, transcendentals=0),
        name="rows_kernel",
    )(band_cut, folded, extra, mirror, fold_tables(), table_y)
    got = lax.all_to_all(rows, ("gx", "gy"), split_axis=0, concat_axis=0, tiled=True)
    pieces = pl.pallas_call(
        field_kernel,
        out_shape=[jax.ShapeDtypeStruct((ROWS, CHUNK), jnp.float32)] * BANDS,
        in_specs=whole(10),
        out_specs=whole(BANDS),
        scratch_shapes=[pltpu.VMEM((ROWS * M, KX + 128), jnp.bfloat16)],
        compiler_params=pltpu.CompilerParams(vmem_limit_bytes=SCRATCH),
        cost_estimate=pl.CostEstimate(flops=3 << 30, bytes_accessed=16 << 20, transcendentals=0),
        name="field_kernel",
    )(scale, got, ensemble[0].transpose(1, 0, 2), column_tables(), *order_tables())
    total = pieces[0]
    for step in range(1, BANDS):
        total = total + lax.ppermute(pieces[step], "band", [(i, (i + step) % BANDS) for i in range(BANDS)])
    return total


def solution(mesh):
    placed = (P("band", None, ("gx", "gy"), None), P("band", None, "gx", "gy", None), P())
    return jax.shard_map(
        body, mesh=mesh, in_specs=placed, out_specs=P(("gx", "gy"), "band"), check_vma=False
    )
```

```python
import functools
import math

import jax
import jax.numpy as jnp
import ml_dtypes
import numpy as np
from jax import lax
from jax.experimental import pallas as pl
from jax.experimental.pallas import tpu as pltpu
from jax.sharding import PartitionSpec as P

NX = 2560
NY = 1408
KX = 1024
KY = 256
M = 16
BANDS = 4
GX = 16
GY = 4
DESTS = GX * GY
ROWS = NY // DESTS
PAD = 24
WAVES = KX // GX
HALF = WAVES // 2
MEMBERS = M // GY
CHUNK = NX // BANDS
SCRATCH = 16 * 1024 * 1024
OWN_FLOPS = 10 ** 10
NEAR_FLOPS = 10 ** 10
ROWS_FLOPS = 2 * 10 ** 10


def low(array):
    return np.asarray(array, dtype=np.float64).astype(ml_dtypes.bfloat16)


def trig(wave, position, period):
    angle = np.mod(np.multiply.outer(wave, position), period) * (2.0 * math.pi / period)
    return np.cos(angle), np.sin(angle)


def first_wave(block):
    return WAVES * (block - GX // 2) if block >= GX // 2 else WAVES * (GX // 2 - 1 - block) + HALF


@functools.lru_cache(None)
def fold_tables():
    fold = np.zeros((2, 2, MEMBERS, HALF, (WAVES + HALF) * MEMBERS))
    for member in range(MEMBERS):
        for pair in range(HALF):
            own = MEMBERS * pair + member
            for part, sign in ((0, 1.0), (1, -1.0)):
                fold[0, part, member, pair, own] = 1.0
                if pair > 0:
                    fold[0, part, member, pair, MEMBERS * (WAVES + HALF - pair) + member] = sign
                fold[1, part, member, pair, MEMBERS * WAVES + own] = 1.0
                fold[1, part, member, pair, MEMBERS * (HALF - pair) + member] = sign
    return low(fold.reshape(2, 2 * MEMBERS * HALF, (WAVES + HALF) * MEMBERS))


@functools.lru_cache(None)
def row_tables():
    cosine, sine = trig(np.arange(NY), np.arange(KY), NY)
    table = np.zeros((GX, GY, PAD, 2 * KY))
    table[:, :, :ROWS] = np.concatenate([cosine, sine], axis=1).reshape(GX, GY, ROWS, 2 * KY)
    firsts = np.arange(DESTS).reshape(GX, GY).T.reshape(-1) * ROWS
    coarse = np.concatenate(trig(firsts, np.arange(KY), NY), axis=1)
    fine = np.stack(trig(np.arange(32), np.arange(KY), NY)).astype(np.float32)
    return low(table.transpose(1, 0, 2, 3).reshape(DESTS * PAD, 2 * KY)), low(coarse), fine


@functools.lru_cache(None)
def column_tables():
    blocks = np.arange(GX).reshape(4, 4).T.reshape(-1)
    waves = np.concatenate([first_wave(block) + np.arange(HALF) for block in blocks])
    columns = np.arange(NX + 2 * CHUNK)
    cosine, sine = trig(waves, columns, NX)
    last = np.zeros((8, columns.size))
    last[0], last[1] = trig(np.array([KX // 2]), columns, NX)
    return low(np.concatenate([cosine, -sine])), low(last).astype(np.float32)


@functools.lru_cache(None)
def order_tables():
    lanes = np.arange(512)
    lane_order = np.zeros((512, 512))
    block, member, pair = lanes // 128, lanes // 32 % 4, lanes % 32
    lane_order[lanes, member * 128 + block * 32 + pair] = 1.0
    row_order = np.zeros((ROWS, GY, MEMBERS, MEMBERS, GY, PAD))
    pick = np.zeros((ROWS, GY, MEMBERS, 2, MEMBERS, 32))
    same = np.zeros((ROWS, GY, MEMBERS, 128))
    for row in range(ROWS):
        for column in range(GY):
            for member in range(MEMBERS):
                row_order[row, column, member, member, column, row] = 1.0
                pick[row, column, member, :, member, row] = 1.0
                same[row, column, member, column:64:GY] = 1.0
    gather = np.zeros((128, GY, GX // 2, PAD))
    lane_part = np.zeros((128, 256))
    join = np.zeros((128, KX))
    spread = np.zeros((128, 256))
    for slot in range(64):
        part, block, column = slot // 32, slot % 32 // GY, slot % GY
        gather[slot, column, block, ROWS] = 1.0
        lane_part[slot, part * 128 : part * 128 + 128] = 1.0
        if block == 0:
            spread[slot, part * 128 : part * 128 + 128] = 1.0
        else:
            other = GX - block
            join[slot, part * 512 + other % 4 * 128 + other // 4 * 32] = 1.0 - 2.0 * part
    return (
        low(lane_order),
        low(row_order.reshape(ROWS * M, MEMBERS * GY * PAD)),
        low(pick.reshape(ROWS * M, 256)),
        same.reshape(ROWS * M, 128).astype(np.float32),
        low(gather.reshape(128, DESTS // 2 * PAD)),
        lane_part.astype(np.float32),
        low(join),
        low(spread),
    )


def nn(a, b):
    return jnp.dot(a, b, preferred_element_type=jnp.float32)


def nt(a, b):
    return lax.dot_general(a, b, (((1,), (1,)), ((), ())), preferred_element_type=jnp.float32)


def place(block, rows):
    negative = (block < GX // 2).astype(jnp.int32)
    return negative, jnp.where(negative == 1, WAVES * (GX // 2 - 1 - block), WAVES * (block - GX // 2))


def pair_mask(base, negative, cut):
    shape = (2 * MEMBERS * HALF, KY)
    wave = base + HALF * negative + (lax.broadcasted_iota(jnp.int32, shape, 0) & (HALF - 1))
    wave_y = lax.broadcasted_iota(jnp.int32, shape, 1)
    return wave * wave + wave_y * wave_y < cut


def own_kernel(cut_ref, own_ref, fold_ref, coarse_ref, fine_ref, folded_ref, extra_ref, scale_ref):
    block = lax.axis_index("gx")
    cut = cut_ref[lax.axis_index("band")]
    negative, base = place(block, WAVES)
    fold = fold_ref[negative, :, : WAVES * MEMBERS]
    inside = pair_mask(base, negative, cut)
    for part in range(2):
        folded_ref[part] = jnp.where(inside, nn(fold, own_ref[part]), 0.0)

    wave_y = lax.broadcasted_iota(jnp.int32, (MEMBERS, KY), 1)
    last = base + WAVES
    edge = last * last + wave_y * wave_y < cut
    edge_real = jnp.where(edge, own_ref[0, :16].astype(jnp.float32)[:MEMBERS], 0.0)
    edge_imag = jnp.where(edge, own_ref[1, :16].astype(jnp.float32)[:MEMBERS], 0.0)
    cosine, sine = fine_ref[0], fine_ref[1]
    even = jnp.concatenate(
        [edge_real[m : m + 1] * cosine - edge_imag[m : m + 1] * sine for m in range(MEMBERS)], axis=0
    )
    odd = jnp.concatenate(
        [edge_real[m : m + 1] * sine + edge_imag[m : m + 1] * cosine for m in range(MEMBERS)], axis=0
    )
    turned = jnp.concatenate(
        [jnp.concatenate([even, -odd], axis=1), jnp.concatenate([odd, even], axis=1)], axis=0
    ).astype(jnp.bfloat16)
    extra_ref[...] = nt(coarse_ref[...], turned)

    shape = (KX, KY)
    wave_x = lax.broadcasted_iota(jnp.int32, shape, 0) - KX // 2
    wave_y = lax.broadcasted_iota(jnp.int32, shape, 1)
    inside = (wave_x * wave_x + wave_y * wave_y < cut).astype(jnp.float32)
    count = jnp.sum(jnp.sum(inside.reshape(KX // 8, 8, KY), axis=0))
    scale_ref[...] = lax.rsqrt(jnp.full((8, 128), count)) * (1.0 / math.sqrt(M * BANDS))


def rows_kernel(cut_ref, folded_ref, extra_ref, mirror_ref, fold_ref, table_ref, out_ref):
    cut = cut_ref[lax.axis_index("band")]
    negative, base = place(lax.axis_index("gx"), WAVES)
    fold = fold_ref[negative, :, WAVES * MEMBERS :]
    inside = pair_mask(base, negative, cut)
    real = folded_ref[0] + jnp.where(inside, nn(fold, mirror_ref[0]), 0.0)
    imag = folded_ref[1] + jnp.where(inside, nn(fold, mirror_ref[1]), 0.0)
    half = MEMBERS * HALF
    with_cosine = jnp.concatenate([real[:half], imag[half:]], axis=0)
    with_sine = jnp.concatenate([-imag[:half], real[half:]], axis=0)
    weights = jnp.concatenate([with_cosine, with_sine], axis=1).astype(jnp.bfloat16)
    dests = DESTS // 4
    row = lax.broadcasted_iota(jnp.int32, (dests, PAD, 256), 1)
    for part in range(4):
        rows = pl.ds(part * dests * PAD, dests * PAD)
        block = nt(table_ref[rows, :], weights).reshape(dests, PAD, 256)
        extra = extra_ref[part * dests : (part + 1) * dests, :].reshape(dests, 1, 256)
        out_ref[rows, :] = jnp.where(row == ROWS, extra, block).reshape(dests * PAD, 256).astype(jnp.bfloat16)


def weigh(alpha, edge, last_ref, start, ensemble_ref, chunk, scale_ref):
    columns = pl.ds(pl.multiple_of(start, CHUNK), CHUNK)
    repeat = CHUNK // 128
    cosine, sine = last_ref[:1, columns], last_ref[1:2, columns]
    alpha = alpha + jnp.concatenate([edge[:, :128]] * repeat, axis=1) * cosine
    alpha = alpha + jnp.concatenate([edge[:, 128:]] * repeat, axis=1) * sine
    fields = ensemble_ref[:, :, pl.ds(pl.multiple_of(chunk * CHUNK, CHUNK), CHUNK)].astype(jnp.float32)
    return jnp.sum(alpha.reshape(ROWS, M, CHUNK) * fields, axis=1) * scale_ref[:1, :1]


def far_kernel(
    scale_ref,
    got_ref,
    ensemble_ref,
    table_ref,
    lane_ref,
    row_ref,
    pick_ref,
    same_ref,
    gather_ref,
    part_ref,
    join_ref,
    spread_ref,
    last_ref,
    joined_ref,
    edge_ref,
    *far_refs,
):
    span = 4 * PAD
    groups = [
        jnp.concatenate(
            [
                got_ref[(4 * column + least) * span : (4 * column + least + 1) * span, part * 128 : part * 128 + 128]
                for least in range(4)
            ],
            axis=1,
        )
        for part in range(2)
        for column in range(GY)
    ]
    ordered = nn(jnp.concatenate(groups, axis=0), lane_ref[...])
    members = []
    for m in range(MEMBERS):
        blocks = []
        for part in range(2):
            for high in range(4):
                starts = [((part * GY + column) * 4 + high) * PAD for column in range(GY)]
                blocks.append(
                    jnp.concatenate([ordered[at : at + PAD, m * 128 : m * 128 + 128] for at in starts], axis=0)
                )
        members.append(jnp.concatenate(blocks, axis=1).astype(jnp.bfloat16))
    sources = GX // 2 * PAD
    edge = nn(
        gather_ref[...],
        jnp.concatenate([got_ref[2 * q * sources : (2 * q + 1) * sources, :] for q in range(GY)], axis=0),
    )
    edge = (nt(pick_ref[...], (edge * part_ref[...]).astype(jnp.bfloat16)) * same_ref[...]).astype(jnp.bfloat16)
    joined = nn(
        jnp.concatenate([row_ref[...], edge], axis=1), jnp.concatenate(members + [join_ref[...]], axis=0)
    ).astype(jnp.bfloat16)
    joined_ref[...] = joined
    edge = nn(edge, spread_ref[...])
    edge_ref[...] = edge
    band = lax.axis_index("band")
    first = lax.rem(band + 1, BANDS) * CHUNK
    alpha = nn(joined, table_ref[:, pl.ds(pl.multiple_of(first, CHUNK), 3 * CHUNK)])
    for step, far_ref in enumerate(far_refs):
        part = alpha[:, step * CHUNK : (step + 1) * CHUNK]
        chunk = lax.rem(band + 1 + step, BANDS)
        far_ref[...] = weigh(part, edge, last_ref, first + step * CHUNK, ensemble_ref, chunk, scale_ref)


def near_kernel(scale_ref, joined_ref, edge_ref, ensemble_ref, table_ref, last_ref, own_ref):
    band = lax.axis_index("band")
    start = pl.multiple_of(band * CHUNK, CHUNK)
    alpha = nn(joined_ref[...], table_ref[:, pl.ds(start, CHUNK)])
    own_ref[...] = weigh(alpha, edge_ref[...], last_ref, start, ensemble_ref, band, scale_ref)


def whole(count):
    return [pl.BlockSpec(memory_space=pltpu.VMEM) for _ in range(count)]


def body(ensemble, spectral, band_cut):
    own = spectral[0].reshape(2, WAVES * MEMBERS, KY)
    mirror = lax.ppermute(own[:, HALF * MEMBERS :], "gx", [(i, GX - 1 - i) for i in range(GX)])
    table_y, coarse, fine = row_tables()
    smem = pl.BlockSpec(memory_space=pltpu.SMEM)
    folded, extra, scale = pl.pallas_call(
        own_kernel,
        out_shape=[
            jax.ShapeDtypeStruct((2, 256, KY), jnp.float32),
            jax.ShapeDtypeStruct((DESTS, 256), jnp.float32),
            jax.ShapeDtypeStruct((8, 128), jnp.float32),
        ],
        in_specs=[smem] + whole(4),
        out_specs=whole(3),
        compiler_params=pltpu.CompilerParams(vmem_limit_bytes=SCRATCH),
        cost_estimate=pl.CostEstimate(flops=OWN_FLOPS, bytes_accessed=1 << 20, transcendentals=0),
        name="own_kernel",
    )(band_cut, own, fold_tables(), coarse, fine)
    rows = pl.pallas_call(
        rows_kernel,
        out_shape=jax.ShapeDtypeStruct((DESTS * PAD, 256), jnp.bfloat16),
        in_specs=[smem] + whole(5),
        out_specs=pl.BlockSpec(memory_space=pltpu.VMEM),
        compiler_params=pltpu.CompilerParams(vmem_limit_bytes=SCRATCH),
        cost_estimate=pl.CostEstimate(flops=ROWS_FLOPS, bytes_accessed=4 << 20, transcendentals=0),
        name="rows_kernel",
    )(band_cut, folded, extra, mirror, fold_tables(), table_y)
    got = lax.all_to_all(rows, ("gy", "gx"), split_axis=0, concat_axis=0, tiled=True)
    fields, (table_x, last) = ensemble[0].transpose(1, 0, 2), column_tables()
    piece = jax.ShapeDtypeStruct((ROWS, CHUNK), jnp.float32)
    joined, edge, *far = pl.pallas_call(
        far_kernel,
        out_shape=[
            jax.ShapeDtypeStruct((ROWS * M, KX), jnp.bfloat16),
            jax.ShapeDtypeStruct((ROWS * M, 256), jnp.float32),
        ]
        + [piece] * (BANDS - 1),
        in_specs=whole(13),
        out_specs=whole(1 + BANDS),
        compiler_params=pltpu.CompilerParams(vmem_limit_bytes=SCRATCH),
        cost_estimate=pl.CostEstimate(flops=3 << 30, bytes_accessed=8 << 20, transcendentals=0),
        name="far_kernel",
    )(scale, got, fields, table_x, *order_tables(), last)
    moved = [ahead(part, step + 1) for step, part in enumerate(far)]
    total = pl.pallas_call(
        near_kernel,
        out_shape=piece,
        in_specs=whole(6),
        out_specs=pl.BlockSpec(memory_space=pltpu.VMEM),
        compiler_params=pltpu.CompilerParams(vmem_limit_bytes=SCRATCH),
        cost_estimate=pl.CostEstimate(flops=NEAR_FLOPS, bytes_accessed=4 << 20, transcendentals=0),
        name="near_kernel",
    )(scale, joined, edge, fields, table_x, last)
    for part in moved:
        total = total + part
    return total


def ahead(piece, step):
    return lax.ppermute(piece, "band", [(i, (i + step) % BANDS) for i in range(BANDS)])


def solution(mesh):
    placed = (P("band", None, ("gx", "gy"), None), P("band", None, "gx", "gy", None), P())
    return jax.shard_map(
        body, mesh=mesh, in_specs=placed, out_specs=P(("gx", "gy"), "band"), check_vma=False
    )
```

```python
import functools
import math

import jax
import jax.numpy as jnp
import ml_dtypes
import numpy as np
from jax import lax
from jax.experimental import pallas as pl
from jax.experimental.pallas import tpu as pltpu
from jax.sharding import PartitionSpec as P

NX = 2560
NY = 1408
KX = 1024
KY = 256
M = 16
BANDS = 4
GX = 16
GY = 4
DESTS = GX * GY
ROWS = NY // DESTS
PAD = 24
WAVES = KX // GX
HALF = WAVES // 2
MEMBERS = M // GY
CHUNK = NX // BANDS
SCRATCH = 16 * 1024 * 1024
OWN_FLOPS = 10 ** 10
NEAR_FLOPS = 10 ** 10
ROWS_FLOPS = 2 * 10 ** 10


def low(array):
    return np.asarray(array, dtype=np.float64).astype(ml_dtypes.bfloat16)


def trig(wave, position, period):
    angle = np.mod(np.multiply.outer(wave, position), period) * (2.0 * math.pi / period)
    return np.cos(angle), np.sin(angle)


def first_wave(block):
    return WAVES * (block - GX // 2) if block >= GX // 2 else WAVES * (GX // 2 - 1 - block) + HALF


@functools.lru_cache(None)
def fold_tables():
    fold = np.zeros((2, 2, MEMBERS, HALF, (WAVES + HALF) * MEMBERS))
    for member in range(MEMBERS):
        for pair in range(HALF):
            own = MEMBERS * pair + member
            for part, sign in ((0, 1.0), (1, -1.0)):
                fold[0, part, member, pair, own] = 1.0
                if pair > 0:
                    fold[0, part, member, pair, MEMBERS * (WAVES + HALF - pair) + member] = sign
                fold[1, part, member, pair, MEMBERS * WAVES + own] = 1.0
                fold[1, part, member, pair, MEMBERS * (HALF - pair) + member] = sign
    return low(fold.reshape(2, 2 * MEMBERS * HALF, (WAVES + HALF) * MEMBERS))


@functools.lru_cache(None)
def row_tables():
    cosine, sine = trig(np.arange(NY), np.arange(KY), NY)
    table = np.zeros((DESTS, PAD, 2 * KY))
    table[:, :ROWS] = np.concatenate([cosine, sine], axis=1).reshape(DESTS, ROWS, 2 * KY)
    coarse = np.concatenate(trig(np.arange(DESTS) * ROWS, np.arange(KY), NY), axis=1)
    fine = np.stack(trig(np.arange(32), np.arange(KY), NY)).astype(np.float32)
    return low(table.reshape(DESTS * PAD, 2 * KY)), low(coarse), fine


@functools.lru_cache(None)
def column_tables():
    waves = np.concatenate([first_wave(block) + np.arange(HALF) for block in range(GX)])
    columns = np.arange(NX + 2 * CHUNK)
    cosine, sine = trig(waves, columns, NX)
    last = np.zeros((8, columns.size))
    last[0], last[1] = trig(np.array([KX // 2]), columns, NX)
    return low(np.concatenate([cosine, -sine])), low(last).astype(np.float32)


@functools.lru_cache(None)
def order_tables():
    row_order = np.zeros((ROWS, GY, MEMBERS, MEMBERS, GY, PAD))
    pick = np.zeros((ROWS, GY, MEMBERS, 2, MEMBERS, 32))
    same = np.zeros((ROWS, GY, MEMBERS, 128))
    for row in range(ROWS):
        for column in range(GY):
            for member in range(MEMBERS):
                row_order[row, column, member, member, column, row] = 1.0
                pick[row, column, member, :, member, row] = 1.0
                same[row, column, member, column:64:GY] = 1.0
    gather = np.zeros((128, GX // 2, GY, PAD))
    lane_part = np.zeros((128, 256))
    join = np.zeros((128, KX))
    spread = np.zeros((128, 256))
    for slot in range(64):
        part, block, column = slot // 32, slot % 32 // GY, slot % GY
        gather[slot, block, column, ROWS] = 1.0
        lane_part[slot, part * 128 : part * 128 + 128] = 1.0
        if block == 0:
            spread[slot, part * 128 : part * 128 + 128] = 1.0
        else:
            other = GX - block
            join[slot, part * 512 + other * 32] = 1.0 - 2.0 * part
    return (
        low(row_order.reshape(ROWS * M, MEMBERS * GY * PAD)),
        low(pick.reshape(ROWS * M, 256)),
        same.reshape(ROWS * M, 128).astype(np.float32),
        low(gather.reshape(128, DESTS // 2 * PAD)),
        lane_part.astype(np.float32),
        low(join),
        low(spread),
    )


def nn(a, b):
    return jnp.dot(a, b, preferred_element_type=jnp.float32)


def nt(a, b):
    return lax.dot_general(a, b, (((1,), (1,)), ((), ())), preferred_element_type=jnp.float32)


def place(block, rows):
    negative = (block < GX // 2).astype(jnp.int32)
    return negative, jnp.where(negative == 1, WAVES * (GX // 2 - 1 - block), WAVES * (block - GX // 2))


def pair_mask(base, negative, cut):
    shape = (2 * MEMBERS * HALF, KY)
    wave = base + HALF * negative + (lax.broadcasted_iota(jnp.int32, shape, 0) & (HALF - 1))
    wave_y = lax.broadcasted_iota(jnp.int32, shape, 1)
    return wave * wave + wave_y * wave_y < cut


def own_kernel(cut_ref, own_ref, fold_ref, coarse_ref, fine_ref, folded_ref, extra_ref, scale_ref):
    block = lax.axis_index("gx")
    cut = cut_ref[lax.axis_index("band")]
    negative, base = place(block, WAVES)
    fold = fold_ref[negative, :, : WAVES * MEMBERS]
    inside = pair_mask(base, negative, cut)
    for part in range(2):
        folded_ref[part] = jnp.where(inside, nn(fold, own_ref[part]), 0.0)

    wave_y = lax.broadcasted_iota(jnp.int32, (MEMBERS, KY), 1)
    last = base + WAVES
    edge = last * last + wave_y * wave_y < cut
    edge_real = jnp.where(edge, own_ref[0, :16].astype(jnp.float32)[:MEMBERS], 0.0)
    edge_imag = jnp.where(edge, own_ref[1, :16].astype(jnp.float32)[:MEMBERS], 0.0)
    cosine, sine = fine_ref[0], fine_ref[1]
    even = jnp.concatenate(
        [edge_real[m : m + 1] * cosine - edge_imag[m : m + 1] * sine for m in range(MEMBERS)], axis=0
    )
    odd = jnp.concatenate(
        [edge_real[m : m + 1] * sine + edge_imag[m : m + 1] * cosine for m in range(MEMBERS)], axis=0
    )
    turned = jnp.concatenate(
        [jnp.concatenate([even, -odd], axis=1), jnp.concatenate([odd, even], axis=1)], axis=0
    ).astype(jnp.bfloat16)
    extra_ref[...] = nt(coarse_ref[...], turned)

    shape = (KX, KY)
    wave_x = lax.broadcasted_iota(jnp.int32, shape, 0) - KX // 2
    wave_y = lax.broadcasted_iota(jnp.int32, shape, 1)
    inside = (wave_x * wave_x + wave_y * wave_y < cut).astype(jnp.float32)
    count = jnp.sum(jnp.sum(inside.reshape(KX // 8, 8, KY), axis=0))
    scale_ref[...] = lax.rsqrt(jnp.full((8, 128), count)) * (1.0 / math.sqrt(M * BANDS))


def rows_kernel(cut_ref, folded_ref, extra_ref, mirror_ref, fold_ref, table_ref, out_ref):
    cut = cut_ref[lax.axis_index("band")]
    negative, base = place(lax.axis_index("gx"), WAVES)
    fold = fold_ref[negative, :, WAVES * MEMBERS :]
    inside = pair_mask(base, negative, cut)
    real = folded_ref[0] + jnp.where(inside, nn(fold, mirror_ref[0]), 0.0)
    imag = folded_ref[1] + jnp.where(inside, nn(fold, mirror_ref[1]), 0.0)
    half = MEMBERS * HALF
    with_cosine = jnp.concatenate([real[:half], imag[half:]], axis=0)
    with_sine = jnp.concatenate([-imag[:half], real[half:]], axis=0)
    weights = jnp.concatenate([with_cosine, with_sine], axis=1).astype(jnp.bfloat16)
    dests = DESTS // 4
    row = lax.broadcasted_iota(jnp.int32, (dests, PAD, 256), 1)
    for part in range(4):
        rows = pl.ds(part * dests * PAD, dests * PAD)
        block = nt(table_ref[rows, :], weights).reshape(dests, PAD, 256)
        extra = extra_ref[part * dests : (part + 1) * dests, :].reshape(dests, 1, 256)
        out_ref[rows, :] = jnp.where(row == ROWS, extra, block).reshape(dests * PAD, 256).astype(jnp.bfloat16)


def weigh(alpha, edge, last_ref, start, ensemble_ref, chunk, scale_ref):
    columns = pl.ds(pl.multiple_of(start, CHUNK), CHUNK)
    repeat = CHUNK // 128
    cosine, sine = last_ref[:1, columns], last_ref[1:2, columns]
    alpha = alpha + jnp.concatenate([edge[:, :128]] * repeat, axis=1) * cosine
    alpha = alpha + jnp.concatenate([edge[:, 128:]] * repeat, axis=1) * sine
    fields = ensemble_ref[:, :, pl.ds(pl.multiple_of(chunk * CHUNK, CHUNK), CHUNK)].astype(jnp.float32)
    return jnp.sum(alpha.reshape(ROWS, M, CHUNK) * fields, axis=1) * scale_ref[:1, :1]


def far_kernel(
    scale_ref,
    got_ref,
    ensemble_ref,
    table_ref,
    row_ref,
    pick_ref,
    same_ref,
    gather_ref,
    part_ref,
    join_ref,
    spread_ref,
    last_ref,
    joined_ref,
    edge_ref,
    *far_refs,
):
    span = GY * PAD
    members = []
    for m in range(MEMBERS):
        pieces = []
        for part in range(2):
            lane = part * 128 + m * HALF
            pieces += [got_ref[block * span : (block + 1) * span, lane : lane + HALF] for block in range(GX)]
        members.append(jnp.concatenate(pieces, axis=1))
    edge = nn(
        gather_ref[...],
        got_ref[: GX // 2 * GY * PAD, :],
    )
    edge = (nt(pick_ref[...], (edge * part_ref[...]).astype(jnp.bfloat16)) * same_ref[...]).astype(jnp.bfloat16)
    joined = nn(
        jnp.concatenate([row_ref[...], edge], axis=1), jnp.concatenate(members + [join_ref[...]], axis=0)
    ).astype(jnp.bfloat16)
    joined_ref[...] = joined
    edge = nn(edge, spread_ref[...])
    edge_ref[...] = edge
    band = lax.axis_index("band")
    first = lax.rem(band + 1, BANDS) * CHUNK
    alpha = nn(joined, table_ref[:, pl.ds(pl.multiple_of(first, CHUNK), 3 * CHUNK)])
    pieces = []
    for step in range(BANDS - 1):
        part = alpha[:, step * CHUNK : (step + 1) * CHUNK]
        chunk = lax.rem(band + 1 + step, BANDS)
        pieces.append(weigh(part, edge, last_ref, first + step * CHUNK, ensemble_ref, chunk, scale_ref))
    odd = (band & 1) == 1
    far_refs[0][...] = jnp.where(odd, pieces[2], pieces[0])
    far_refs[1][...] = jnp.where(odd, pieces[0], pieces[2])
    far_refs[2][...] = pieces[1]


def near_kernel(scale_ref, joined_ref, edge_ref, ensemble_ref, table_ref, last_ref, own_ref):
    band = lax.axis_index("band")
    start = pl.multiple_of(band * CHUNK, CHUNK)
    alpha = nn(joined_ref[...], table_ref[:, pl.ds(start, CHUNK)])
    own_ref[...] = weigh(alpha, edge_ref[...], last_ref, start, ensemble_ref, band, scale_ref)


def whole(count):
    return [pl.BlockSpec(memory_space=pltpu.VMEM) for _ in range(count)]


def body(ensemble, spectral, band_cut):
    own = spectral[0].reshape(2, WAVES * MEMBERS, KY)
    mirror = lax.ppermute(own[:, HALF * MEMBERS :], "gx", [(i, GX - 1 - i) for i in range(GX)])
    table_y, coarse, fine = row_tables()
    smem = pl.BlockSpec(memory_space=pltpu.SMEM)
    folded, extra, scale = pl.pallas_call(
        own_kernel,
        out_shape=[
            jax.ShapeDtypeStruct((2, 256, KY), jnp.float32),
            jax.ShapeDtypeStruct((DESTS, 256), jnp.float32),
            jax.ShapeDtypeStruct((8, 128), jnp.float32),
        ],
        in_specs=[smem] + whole(4),
        out_specs=whole(3),
        compiler_params=pltpu.CompilerParams(vmem_limit_bytes=SCRATCH),
        cost_estimate=pl.CostEstimate(flops=OWN_FLOPS, bytes_accessed=1 << 20, transcendentals=0),
        name="own_kernel",
    )(band_cut, own, fold_tables(), coarse, fine)
    rows = pl.pallas_call(
        rows_kernel,
        out_shape=jax.ShapeDtypeStruct((DESTS * PAD, 256), jnp.bfloat16),
        in_specs=[smem] + whole(5),
        out_specs=pl.BlockSpec(memory_space=pltpu.VMEM),
        compiler_params=pltpu.CompilerParams(vmem_limit_bytes=SCRATCH),
        cost_estimate=pl.CostEstimate(flops=ROWS_FLOPS, bytes_accessed=4 << 20, transcendentals=0),
        name="rows_kernel",
    )(band_cut, folded, extra, mirror, fold_tables(), table_y)
    got = lax.all_to_all(rows, ("gx", "gy"), split_axis=0, concat_axis=0, tiled=True)
    fields, (table_x, last) = ensemble[0].transpose(1, 0, 2), column_tables()
    piece = jax.ShapeDtypeStruct((ROWS, CHUNK), jnp.float32)
    joined, edge, *far = pl.pallas_call(
        far_kernel,
        out_shape=[
            jax.ShapeDtypeStruct((ROWS * M, KX), jnp.bfloat16),
            jax.ShapeDtypeStruct((ROWS * M, 256), jnp.float32),
        ]
        + [piece] * (BANDS - 1),
        in_specs=whole(12),
        out_specs=whole(1 + BANDS),
        compiler_params=pltpu.CompilerParams(vmem_limit_bytes=SCRATCH),
        cost_estimate=pl.CostEstimate(flops=3 << 30, bytes_accessed=8 << 20, transcendentals=0),
        name="far_kernel",
    )(scale, got, fields, table_x, *order_tables(), last)
    moved = [ahead(part, flip) for flip, part in zip((2, 3, 1), (far[2], far[1], far[0]))]
    total = pl.pallas_call(
        near_kernel,
        out_shape=piece,
        in_specs=whole(6),
        out_specs=pl.BlockSpec(memory_space=pltpu.VMEM),
        compiler_params=pltpu.CompilerParams(vmem_limit_bytes=SCRATCH),
        cost_estimate=pl.CostEstimate(flops=NEAR_FLOPS, bytes_accessed=4 << 20, transcendentals=0),
        name="near_kernel",
    )(scale, joined, edge, fields, table_x, last)
    for part in moved:
        total = total + part
    return total


def ahead(piece, step):
    return lax.ppermute(piece, "band", [(i, i ^ step) for i in range(BANDS)])


def solution(mesh):
    placed = (P("band", None, ("gx", "gy"), None), P("band", None, "gx", "gy", None), P())
    return jax.shard_map(
        body, mesh=mesh, in_specs=placed, out_specs=P(("gx", "gy"), "band"), check_vma=False
    )
```

```python
import functools
import math

import jax
import jax.numpy as jnp
import ml_dtypes
import numpy as np
from jax import lax
from jax.experimental import pallas as pl
from jax.experimental.pallas import tpu as pltpu
from jax.sharding import PartitionSpec as P

NX = 2560
NY = 1408
KX = 1024
KY = 256
M = 16
BANDS = 4
GX = 16
GY = 4
DESTS = GX * GY
ROWS = NY // DESTS
PAD = 24
WAVES = KX // GX
HALF = WAVES // 2
MEMBERS = M // GY
CHUNK = NX // BANDS
SENT = jnp.bfloat16
SCRATCH = 16 * 1024 * 1024
OWN_FLOPS = 10 ** 10
NEAR_FLOPS = 10 ** 10
ROWS_FLOPS = 2 * 10 ** 10


def low(array):
    return np.asarray(array, dtype=np.float64).astype(ml_dtypes.bfloat16)


def trig(wave, position, period):
    angle = np.mod(np.multiply.outer(wave, position), period) * (2.0 * math.pi / period)
    return np.cos(angle), np.sin(angle)


def first_wave(block):
    return WAVES * (block - GX // 2) if block >= GX // 2 else WAVES * (GX // 2 - 1 - block) + HALF


@functools.lru_cache(None)
def fold_tables():
    fold = np.zeros((2, 2, MEMBERS, HALF, (WAVES + HALF) * MEMBERS))
    for member in range(MEMBERS):
        for pair in range(HALF):
            own = MEMBERS * pair + member
            for part, sign in ((0, 1.0), (1, -1.0)):
                fold[0, part, member, pair, own] = 1.0
                if pair > 0:
                    fold[0, part, member, pair, MEMBERS * (WAVES + HALF - pair) + member] = sign
                fold[1, part, member, pair, MEMBERS * WAVES + own] = 1.0
                fold[1, part, member, pair, MEMBERS * (HALF - pair) + member] = sign
    return low(fold.reshape(2, 2 * MEMBERS * HALF, (WAVES + HALF) * MEMBERS))


@functools.lru_cache(None)
def row_tables():
    cosine, sine = trig(np.arange(NY), np.arange(KY), NY)
    table = np.zeros((DESTS, PAD, 2 * KY))
    table[:, :ROWS] = np.concatenate([cosine, sine], axis=1).reshape(DESTS, ROWS, 2 * KY)
    coarse = np.concatenate(trig(np.arange(DESTS) * ROWS, np.arange(KY), NY), axis=1)
    fine = np.stack(trig(np.arange(32), np.arange(KY), NY)).astype(np.float32)
    return low(table.reshape(DESTS * PAD, 2 * KY)), low(coarse), fine


@functools.lru_cache(None)
def column_tables():
    waves = np.concatenate([first_wave(block) + np.arange(HALF) for block in range(GX)])
    columns = np.arange(NX + 2 * CHUNK)
    cosine, sine = trig(waves, columns, NX)
    last = np.zeros((8, columns.size))
    last[0], last[1] = trig(np.array([KX // 2]), columns, NX)
    return low(np.concatenate([cosine, -sine])), low(last).astype(np.float32)


@functools.lru_cache(None)
def order_tables():
    row_order = np.zeros((ROWS, GY, MEMBERS, MEMBERS, GY, PAD))
    pick = np.zeros((ROWS, GY, MEMBERS, 2, MEMBERS, 32))
    same = np.zeros((ROWS, GY, MEMBERS, 128))
    for row in range(ROWS):
        for column in range(GY):
            for member in range(MEMBERS):
                row_order[row, column, member, member, column, row] = 1.0
                pick[row, column, member, :, member, row] = 1.0
                same[row, column, member, column:64:GY] = 1.0
    gather = np.zeros((128, GX // 2, GY, PAD))
    lane_part = np.zeros((128, 256))
    join = np.zeros((128, KX))
    spread = np.zeros((128, 256))
    for slot in range(64):
        part, block, column = slot // 32, slot % 32 // GY, slot % GY
        gather[slot, block, column, ROWS] = 1.0
        lane_part[slot, part * 128 : part * 128 + 128] = 1.0
        if block == 0:
            spread[slot, part * 128 : part * 128 + 128] = 1.0
        else:
            other = GX - block
            join[slot, part * 512 + other * 32] = 1.0 - 2.0 * part
    return (
        low(row_order.reshape(ROWS * M, MEMBERS * GY * PAD)),
        low(pick.reshape(ROWS * M, 256)),
        same.reshape(ROWS * M, 128).astype(np.float32),
        low(gather.reshape(128, DESTS // 2 * PAD)),
        lane_part.astype(np.float32),
        low(join),
        low(spread),
    )


def nn(a, b):
    return jnp.dot(a, b, preferred_element_type=jnp.float32)


def nt(a, b):
    return lax.dot_general(a, b, (((1,), (1,)), ((), ())), preferred_element_type=jnp.float32)


def place(block, rows):
    negative = (block < GX // 2).astype(jnp.int32)
    return negative, jnp.where(negative == 1, WAVES * (GX // 2 - 1 - block), WAVES * (block - GX // 2))


def pair_mask(base, negative, cut):
    shape = (2 * MEMBERS * HALF, KY)
    wave = base + HALF * negative + (lax.broadcasted_iota(jnp.int32, shape, 0) & (HALF - 1))
    wave_y = lax.broadcasted_iota(jnp.int32, shape, 1)
    return wave * wave + wave_y * wave_y < cut


def own_kernel(cut_ref, own_ref, fold_ref, coarse_ref, fine_ref, folded_ref, extra_ref, scale_ref):
    block = lax.axis_index("gx")
    cut = cut_ref[lax.axis_index("band")]
    negative, base = place(block, WAVES)
    fold = fold_ref[negative, :, : WAVES * MEMBERS]
    inside = pair_mask(base, negative, cut)
    for part in range(2):
        folded_ref[part] = jnp.where(inside, nn(fold, own_ref[part]), 0.0)

    wave_y = lax.broadcasted_iota(jnp.int32, (MEMBERS, KY), 1)
    last = base + WAVES
    edge = last * last + wave_y * wave_y < cut
    edge_real = jnp.where(edge, own_ref[0, :16].astype(jnp.float32)[:MEMBERS], 0.0)
    edge_imag = jnp.where(edge, own_ref[1, :16].astype(jnp.float32)[:MEMBERS], 0.0)
    cosine, sine = fine_ref[0], fine_ref[1]
    even = jnp.concatenate(
        [edge_real[m : m + 1] * cosine - edge_imag[m : m + 1] * sine for m in range(MEMBERS)], axis=0
    )
    odd = jnp.concatenate(
        [edge_real[m : m + 1] * sine + edge_imag[m : m + 1] * cosine for m in range(MEMBERS)], axis=0
    )
    turned = jnp.concatenate(
        [jnp.concatenate([even, -odd], axis=1), jnp.concatenate([odd, even], axis=1)], axis=0
    ).astype(jnp.bfloat16)
    extra_ref[...] = nt(coarse_ref[...], turned)

    shape = (KX, KY)
    wave_x = lax.broadcasted_iota(jnp.int32, shape, 0) - KX // 2
    wave_y = lax.broadcasted_iota(jnp.int32, shape, 1)
    inside = (wave_x * wave_x + wave_y * wave_y < cut).astype(jnp.float32)
    count = jnp.sum(jnp.sum(inside.reshape(KX // 8, 8, KY), axis=0))
    scale_ref[...] = lax.rsqrt(jnp.full((8, 128), count)) * (1.0 / math.sqrt(M * BANDS))


def rows_kernel(cut_ref, folded_ref, extra_ref, mirror_ref, fold_ref, table_ref, out_ref):
    cut = cut_ref[lax.axis_index("band")]
    negative, base = place(lax.axis_index("gx"), WAVES)
    fold = fold_ref[negative, :, WAVES * MEMBERS :]
    inside = pair_mask(base, negative, cut)
    real = folded_ref[0] + jnp.where(inside, nn(fold, mirror_ref[0]), 0.0)
    imag = folded_ref[1] + jnp.where(inside, nn(fold, mirror_ref[1]), 0.0)
    half = MEMBERS * HALF
    with_cosine = jnp.concatenate([real[:half], imag[half:]], axis=0)
    with_sine = jnp.concatenate([-imag[:half], real[half:]], axis=0)
    weights = jnp.concatenate([with_cosine, with_sine], axis=1).astype(jnp.bfloat16)
    dests = DESTS // 4
    row = lax.broadcasted_iota(jnp.int32, (dests, PAD, 256), 1)
    for part in range(4):
        rows = pl.ds(part * dests * PAD, dests * PAD)
        block = nt(table_ref[rows, :], weights).reshape(dests, PAD, 256)
        extra = extra_ref[part * dests : (part + 1) * dests, :].reshape(dests, 1, 256)
        out_ref[rows, :] = jnp.where(row == ROWS, extra, block).reshape(dests * PAD, 256).astype(jnp.bfloat16)


def weigh(alpha, edge, last_ref, start, ensemble_ref, chunk, scale_ref):
    columns = pl.ds(pl.multiple_of(start, CHUNK), CHUNK)
    repeat = CHUNK // 128
    cosine, sine = last_ref[:1, columns], last_ref[1:2, columns]
    alpha = alpha + jnp.concatenate([edge[:, :128]] * repeat, axis=1) * cosine
    alpha = alpha + jnp.concatenate([edge[:, 128:]] * repeat, axis=1) * sine
    fields = ensemble_ref[:, :, pl.ds(pl.multiple_of(chunk * CHUNK, CHUNK), CHUNK)].astype(jnp.float32)
    return jnp.sum(alpha.reshape(ROWS, M, CHUNK) * fields, axis=1) * scale_ref[:1, :1]


def far_kernel(
    scale_ref,
    got_ref,
    ensemble_ref,
    table_ref,
    row_ref,
    pick_ref,
    same_ref,
    gather_ref,
    part_ref,
    join_ref,
    spread_ref,
    last_ref,
    joined_ref,
    edge_ref,
    relay_ref,
):
    span = GY * PAD
    members = []
    for m in range(MEMBERS):
        pieces = []
        for part in range(2):
            lane = part * 128 + m * HALF
            pieces += [got_ref[block * span : (block + 1) * span, lane : lane + HALF] for block in range(GX)]
        members.append(jnp.concatenate(pieces, axis=1))
    edge = nn(
        gather_ref[...],
        got_ref[: GX // 2 * GY * PAD, :],
    )
    edge = (nt(pick_ref[...], (edge * part_ref[...]).astype(jnp.bfloat16)) * same_ref[...]).astype(jnp.bfloat16)
    joined = nn(
        jnp.concatenate([row_ref[...], edge], axis=1), jnp.concatenate(members + [join_ref[...]], axis=0)
    ).astype(jnp.bfloat16)
    joined_ref[...] = joined
    edge = nn(edge, spread_ref[...])
    edge_ref[...] = edge
    chunk = BANDS - 1 - (lax.axis_index("band") ^ 1)
    start = pl.multiple_of(chunk * CHUNK, CHUNK)
    alpha = nn(joined, table_ref[:, pl.ds(start, CHUNK)])
    relay_ref[...] = weigh(alpha, edge, last_ref, start, ensemble_ref, chunk, scale_ref).astype(relay_ref.dtype)


def near_kernel(
    scale_ref, joined_ref, edge_ref, ensemble_ref, table_ref, last_ref, direct_ref, mirrored_ref, own_ref
):
    band = lax.axis_index("band")
    after = BANDS - (band ^ 1)
    first = lax.rem(after, BANDS) * CHUNK
    alpha = nn(joined_ref[...], table_ref[:, pl.ds(pl.multiple_of(first, CHUNK), 3 * CHUNK)])
    pieces = []
    for step in range(BANDS - 1):
        part = alpha[:, step * CHUNK : (step + 1) * CHUNK]
        chunk = lax.rem(after + step, BANDS)
        pieces.append(weigh(part, edge_ref[...], last_ref, first + step * CHUNK, ensemble_ref, chunk, scale_ref))
    odd = (band & 1) == 1
    direct_ref[...] = jnp.where(odd, pieces[0], pieces[2]).astype(direct_ref.dtype)
    mirrored_ref[...] = jnp.where(odd, pieces[2], pieces[0])
    own_ref[...] = pieces[1]


def whole(count):
    return [pl.BlockSpec(memory_space=pltpu.VMEM) for _ in range(count)]


def body(ensemble, spectral, band_cut):
    own = spectral[0].reshape(2, WAVES * MEMBERS, KY)
    mirror = lax.ppermute(own[:, HALF * MEMBERS :], "gx", [(i, GX - 1 - i) for i in range(GX)])
    table_y, coarse, fine = row_tables()
    smem = pl.BlockSpec(memory_space=pltpu.SMEM)
    folded, extra, scale = pl.pallas_call(
        own_kernel,
        out_shape=[
            jax.ShapeDtypeStruct((2, 256, KY), jnp.float32),
            jax.ShapeDtypeStruct((DESTS, 256), jnp.float32),
            jax.ShapeDtypeStruct((8, 128), jnp.float32),
        ],
        in_specs=[smem] + whole(4),
        out_specs=whole(3),
        compiler_params=pltpu.CompilerParams(vmem_limit_bytes=SCRATCH),
        cost_estimate=pl.CostEstimate(flops=OWN_FLOPS, bytes_accessed=1 << 20, transcendentals=0),
        name="own_kernel",
    )(band_cut, own, fold_tables(), coarse, fine)
    rows = pl.pallas_call(
        rows_kernel,
        out_shape=jax.ShapeDtypeStruct((DESTS * PAD, 256), jnp.bfloat16),
        in_specs=[smem] + whole(5),
        out_specs=pl.BlockSpec(memory_space=pltpu.VMEM),
        compiler_params=pltpu.CompilerParams(vmem_limit_bytes=SCRATCH),
        cost_estimate=pl.CostEstimate(flops=ROWS_FLOPS, bytes_accessed=4 << 20, transcendentals=0),
        name="rows_kernel",
    )(band_cut, folded, extra, mirror, fold_tables(), table_y)
    got = lax.all_to_all(rows, ("gx", "gy"), split_axis=0, concat_axis=0, tiled=True)
    fields, (table_x, last) = ensemble[0].transpose(1, 0, 2), column_tables()
    piece = jax.ShapeDtypeStruct((ROWS, CHUNK), jnp.float32)
    sent = jax.ShapeDtypeStruct((ROWS, CHUNK), SENT)
    joined, edge, relay = pl.pallas_call(
        far_kernel,
        out_shape=[
            jax.ShapeDtypeStruct((ROWS * M, KX), jnp.bfloat16),
            jax.ShapeDtypeStruct((ROWS * M, 256), jnp.float32),
            sent,
        ],
        in_specs=whole(12),
        out_specs=whole(3),
        compiler_params=pltpu.CompilerParams(vmem_limit_bytes=SCRATCH),
        cost_estimate=pl.CostEstimate(flops=3 << 30, bytes_accessed=8 << 20, transcendentals=0),
        name="far_kernel",
    )(scale, got, fields, table_x, *order_tables(), last)
    relay = ahead(relay, 1)
    direct, mirrored, own = pl.pallas_call(
        near_kernel,
        out_shape=[sent, piece, piece],
        in_specs=whole(6),
        out_specs=whole(3),
        compiler_params=pltpu.CompilerParams(vmem_limit_bytes=SCRATCH),
        cost_estimate=pl.CostEstimate(flops=NEAR_FLOPS, bytes_accessed=4 << 20, transcendentals=0),
        name="near_kernel",
    )(scale, joined, edge, fields, table_x, last)
    direct = ahead(direct, 1)
    across = ahead((mirrored + relay.astype(jnp.float32)).astype(SENT), 3)
    return (own + direct.astype(jnp.float32)) + across.astype(jnp.float32)


def ahead(piece, step):
    return lax.ppermute(piece, "band", [(i, i ^ step) for i in range(BANDS)])


def solution(mesh):
    placed = (P("band", None, ("gx", "gy"), None), P("band", None, "gx", "gy", None), P())
    return jax.shard_map(
        body, mesh=mesh, in_specs=placed, out_specs=P(("gx", "gy"), "band"), check_vma=False
    )
```

```python
import functools
import math

import jax
import jax.numpy as jnp
import ml_dtypes
import numpy as np
from jax import lax
from jax.experimental import pallas as pl
from jax.experimental.pallas import tpu as pltpu
from jax.sharding import PartitionSpec as P

NX = 2560
NY = 1408
KX = 1024
KY = 256
M = 16
BANDS = 4
GX = 16
GY = 4
DESTS = GX * GY
ROWS = NY // DESTS
PAD = 24
WAVES = KX // GX
HALF = WAVES // 2
MEMBERS = M // GY
CHUNK = NX // BANDS
SENT = jnp.bfloat16
SCRATCH = 16 * 1024 * 1024
OWN_FLOPS = 10 ** 10
NEAR_FLOPS = 10 ** 10
ROWS_FLOPS = 2 * 10 ** 10


def low(array):
    return np.asarray(array, dtype=np.float64).astype(ml_dtypes.bfloat16)


def trig(wave, position, period):
    angle = np.mod(np.multiply.outer(wave, position), period) * (2.0 * math.pi / period)
    return np.cos(angle), np.sin(angle)


def first_wave(block):
    return WAVES * (block - GX // 2) if block >= GX // 2 else WAVES * (GX // 2 - 1 - block) + HALF


@functools.lru_cache(None)
def fold_tables():
    fold = np.zeros((2, 2, MEMBERS, HALF, (WAVES + HALF) * MEMBERS))
    for member in range(MEMBERS):
        for pair in range(HALF):
            own = MEMBERS * pair + member
            for part, sign in ((0, 1.0), (1, -1.0)):
                fold[0, part, member, pair, own] = 1.0
                if pair > 0:
                    fold[0, part, member, pair, MEMBERS * (WAVES + HALF - pair) + member] = sign
                fold[1, part, member, pair, MEMBERS * WAVES + own] = 1.0
                fold[1, part, member, pair, MEMBERS * (HALF - pair) + member] = sign
    return low(fold.reshape(2, 2 * MEMBERS * HALF, (WAVES + HALF) * MEMBERS))


@functools.lru_cache(None)
def row_tables():
    cosine, sine = trig(np.arange(NY), np.arange(KY), NY)
    table = np.zeros((DESTS, PAD, 2 * KY))
    table[:, :ROWS] = np.concatenate([cosine, sine], axis=1).reshape(DESTS, ROWS, 2 * KY)
    coarse = np.concatenate(trig(np.arange(DESTS) * ROWS, np.arange(KY), NY), axis=1)
    fine = np.stack(trig(np.arange(32), np.arange(KY), NY)).astype(np.float32)
    return low(table.reshape(DESTS * PAD, 2 * KY)), low(coarse), fine


@functools.lru_cache(None)
def column_tables():
    waves = np.concatenate([first_wave(block) + np.arange(HALF) for block in range(GX)])
    columns = np.arange(NX + 2 * CHUNK)
    cosine, sine = trig(waves, columns, NX)
    last = np.zeros((8, columns.size))
    last[0], last[1] = trig(np.array([KX // 2]), columns, NX)
    return low(np.concatenate([cosine, -sine])), low(last).astype(np.float32)


@functools.lru_cache(None)
def order_tables():
    row_order = np.zeros((ROWS, GY, MEMBERS, MEMBERS, GY, PAD))
    pick = np.zeros((ROWS, GY, MEMBERS, 2, MEMBERS, 32))
    same = np.zeros((ROWS, GY, MEMBERS, 128))
    for row in range(ROWS):
        for column in range(GY):
            for member in range(MEMBERS):
                row_order[row, column, member, member, column, row] = 1.0
                pick[row, column, member, :, member, row] = 1.0
                same[row, column, member, column:64:GY] = 1.0
    gather = np.zeros((128, GX // 2, GY, PAD))
    lane_part = np.zeros((128, 256))
    join = np.zeros((128, KX))
    spread = np.zeros((128, 256))
    for slot in range(64):
        part, block, column = slot // 32, slot % 32 // GY, slot % GY
        gather[slot, block, column, ROWS] = 1.0
        lane_part[slot, part * 128 : part * 128 + 128] = 1.0
        if block == 0:
            spread[slot, part * 128 : part * 128 + 128] = 1.0
        else:
            other = GX - block
            join[slot, part * 512 + other * 32] = 1.0 - 2.0 * part
    return (
        low(row_order.reshape(ROWS * M, MEMBERS * GY * PAD)),
        low(pick.reshape(ROWS * M, 256)),
        same.reshape(ROWS * M, 128).astype(np.float32),
        low(gather.reshape(128, DESTS // 2 * PAD)),
        lane_part.astype(np.float32),
        low(join),
        low(spread),
    )


def nn(a, b):
    return jnp.dot(a, b, preferred_element_type=jnp.float32)


def nt(a, b):
    return lax.dot_general(a, b, (((1,), (1,)), ((), ())), preferred_element_type=jnp.float32)


def place(block, rows):
    negative = (block < GX // 2).astype(jnp.int32)
    return negative, jnp.where(negative == 1, WAVES * (GX // 2 - 1 - block), WAVES * (block - GX // 2))


def pair_mask(base, negative, cut):
    shape = (2 * MEMBERS * HALF, KY)
    wave = base + HALF * negative + (lax.broadcasted_iota(jnp.int32, shape, 0) & (HALF - 1))
    wave_y = lax.broadcasted_iota(jnp.int32, shape, 1)
    return wave * wave + wave_y * wave_y < cut


def own_kernel(cut_ref, own_ref, fold_ref, coarse_ref, fine_ref, folded_ref, extra_ref, scale_ref):
    block = lax.axis_index("gx")
    cut = cut_ref[lax.axis_index("band")]
    negative, base = place(block, WAVES)
    fold = fold_ref[negative, :, : WAVES * MEMBERS]
    inside = pair_mask(base, negative, cut)
    for part in range(2):
        folded_ref[part] = jnp.where(inside, nn(fold, own_ref[part]), 0.0)

    wave_y = lax.broadcasted_iota(jnp.int32, (MEMBERS, KY), 1)
    last = base + WAVES
    edge = last * last + wave_y * wave_y < cut
    edge_real = jnp.where(edge, own_ref[0, :16].astype(jnp.float32)[:MEMBERS], 0.0)
    edge_imag = jnp.where(edge, own_ref[1, :16].astype(jnp.float32)[:MEMBERS], 0.0)
    cosine, sine = fine_ref[0], fine_ref[1]
    even = jnp.concatenate(
        [edge_real[m : m + 1] * cosine - edge_imag[m : m + 1] * sine for m in range(MEMBERS)], axis=0
    )
    odd = jnp.concatenate(
        [edge_real[m : m + 1] * sine + edge_imag[m : m + 1] * cosine for m in range(MEMBERS)], axis=0
    )
    turned = jnp.concatenate(
        [jnp.concatenate([even, -odd], axis=1), jnp.concatenate([odd, even], axis=1)], axis=0
    ).astype(jnp.bfloat16)
    extra_ref[...] = nt(coarse_ref[...], turned)

    shape = (KX, KY)
    wave_x = lax.broadcasted_iota(jnp.int32, shape, 0) - KX // 2
    wave_y = lax.broadcasted_iota(jnp.int32, shape, 1)
    inside = (wave_x * wave_x + wave_y * wave_y < cut).astype(jnp.float32)
    count = jnp.sum(jnp.sum(inside.reshape(KX // 8, 8, KY), axis=0))
    scale_ref[...] = lax.rsqrt(jnp.full((8, 128), count)) * (1.0 / math.sqrt(M * BANDS))


def rows_kernel(cut_ref, folded_ref, extra_ref, mirror_ref, fold_ref, table_ref, out_ref):
    cut = cut_ref[lax.axis_index("band")]
    negative, base = place(lax.axis_index("gx"), WAVES)
    fold = fold_ref[negative, :, WAVES * MEMBERS :]
    inside = pair_mask(base, negative, cut)
    real = folded_ref[0] + jnp.where(inside, nn(fold, mirror_ref[0]), 0.0)
    imag = folded_ref[1] + jnp.where(inside, nn(fold, mirror_ref[1]), 0.0)
    half = MEMBERS * HALF
    with_cosine = jnp.concatenate([real[:half], imag[half:]], axis=0)
    with_sine = jnp.concatenate([-imag[:half], real[half:]], axis=0)
    weights = jnp.concatenate([with_cosine, with_sine], axis=1).astype(jnp.bfloat16)
    dests = DESTS // 4
    row = lax.broadcasted_iota(jnp.int32, (dests, PAD, 256), 1)
    for part in range(4):
        rows = pl.ds(part * dests * PAD, dests * PAD)
        block = nt(table_ref[rows, :], weights).reshape(dests, PAD, 256)
        extra = extra_ref[part * dests : (part + 1) * dests, :].reshape(dests, 1, 256)
        out_ref[rows, :] = jnp.where(row == ROWS, extra, block).reshape(dests * PAD, 256).astype(jnp.bfloat16)


def weigh(alpha, edge, last_ref, start, ensemble_ref, chunk, scale_ref):
    columns = pl.ds(pl.multiple_of(start, CHUNK), CHUNK)
    repeat = CHUNK // 128
    cosine, sine = last_ref[:1, columns], last_ref[1:2, columns]
    alpha = alpha + jnp.concatenate([edge[:, :128]] * repeat, axis=1) * cosine
    alpha = alpha + jnp.concatenate([edge[:, 128:]] * repeat, axis=1) * sine
    fields = ensemble_ref[:, :, pl.ds(pl.multiple_of(chunk * CHUNK, CHUNK), CHUNK)].astype(jnp.float32)
    return jnp.sum(alpha.reshape(ROWS, M, CHUNK) * fields, axis=1) * scale_ref[:1, :1]


def far_kernel(
    scale_ref,
    got_ref,
    ensemble_ref,
    table_ref,
    row_ref,
    pick_ref,
    same_ref,
    gather_ref,
    part_ref,
    join_ref,
    spread_ref,
    last_ref,
    joined_ref,
    edge_ref,
    relay_ref,
):
    span = GY * PAD
    members = []
    for m in range(MEMBERS):
        pieces = []
        for part in range(2):
            lane = part * 128 + m * HALF
            pieces += [got_ref[block * span : (block + 1) * span, lane : lane + HALF] for block in range(GX)]
        members.append(jnp.concatenate(pieces, axis=1))
    edge = nn(
        gather_ref[...],
        got_ref[: GX // 2 * GY * PAD, :],
    )
    edge = (nt(pick_ref[...], (edge * part_ref[...]).astype(jnp.bfloat16)) * same_ref[...]).astype(jnp.bfloat16)
    joined = nn(
        jnp.concatenate([row_ref[...], edge], axis=1), jnp.concatenate(members + [join_ref[...]], axis=0)
    ).astype(jnp.bfloat16)
    joined_ref[...] = joined
    edge = nn(edge, spread_ref[...])
    edge_ref[...] = edge
    chunk = BANDS - 1 - (lax.axis_index("band") ^ 1)
    start = pl.multiple_of(chunk * CHUNK, CHUNK)
    alpha = nn(joined, table_ref[:, pl.ds(start, CHUNK)])
    relay_ref[...] = weigh(alpha, edge, last_ref, start, ensemble_ref, chunk, scale_ref).astype(relay_ref.dtype)


def chunk_field(chunk, joined, edge, last_ref, ensemble_ref, table_ref, scale_ref):
    start = pl.multiple_of(chunk * CHUNK, CHUNK)
    alpha = nn(joined, table_ref[:, pl.ds(start, CHUNK)])
    return weigh(alpha, edge, last_ref, start, ensemble_ref, chunk, scale_ref)


def near_kernel(scale_ref, joined_ref, edge_ref, ensemble_ref, table_ref, last_ref, direct_ref, mirrored_ref):
    band = lax.axis_index("band")
    refs = (last_ref, ensemble_ref, table_ref, scale_ref)
    joined, edge = joined_ref[...], edge_ref[...]
    mirrored_ref[...] = chunk_field(BANDS - 1 - band, joined, edge, *refs)
    direct_ref[...] = chunk_field(band ^ 1, joined, edge, *refs).astype(direct_ref.dtype)


def own_field_kernel(scale_ref, joined_ref, edge_ref, ensemble_ref, table_ref, last_ref, own_ref):
    band = lax.axis_index("band")
    own_ref[...] = chunk_field(
        band, joined_ref[...], edge_ref[...], last_ref, ensemble_ref, table_ref, scale_ref
    )


def whole(count):
    return [pl.BlockSpec(memory_space=pltpu.VMEM) for _ in range(count)]


def body(ensemble, spectral, band_cut):
    own = spectral[0].reshape(2, WAVES * MEMBERS, KY)
    mirror = lax.ppermute(own[:, HALF * MEMBERS :], "gx", [(i, GX - 1 - i) for i in range(GX)])
    table_y, coarse, fine = row_tables()
    smem = pl.BlockSpec(memory_space=pltpu.SMEM)
    folded, extra, scale = pl.pallas_call(
        own_kernel,
        out_shape=[
            jax.ShapeDtypeStruct((2, 256, KY), jnp.float32),
            jax.ShapeDtypeStruct((DESTS, 256), jnp.float32),
            jax.ShapeDtypeStruct((8, 128), jnp.float32),
        ],
        in_specs=[smem] + whole(4),
        out_specs=whole(3),
        compiler_params=pltpu.CompilerParams(vmem_limit_bytes=SCRATCH),
        cost_estimate=pl.CostEstimate(flops=OWN_FLOPS, bytes_accessed=1 << 20, transcendentals=0),
        name="own_kernel",
    )(band_cut, own, fold_tables(), coarse, fine)
    rows = pl.pallas_call(
        rows_kernel,
        out_shape=jax.ShapeDtypeStruct((DESTS * PAD, 256), jnp.bfloat16),
        in_specs=[smem] + whole(5),
        out_specs=pl.BlockSpec(memory_space=pltpu.VMEM),
        compiler_params=pltpu.CompilerParams(vmem_limit_bytes=SCRATCH),
        cost_estimate=pl.CostEstimate(flops=ROWS_FLOPS, bytes_accessed=4 << 20, transcendentals=0),
        name="rows_kernel",
    )(band_cut, folded, extra, mirror, fold_tables(), table_y)
    got = lax.all_to_all(rows, ("gx", "gy"), split_axis=0, concat_axis=0, tiled=True)
    fields, (table_x, last) = ensemble[0].transpose(1, 0, 2), column_tables()
    piece = jax.ShapeDtypeStruct((ROWS, CHUNK), jnp.float32)
    sent = jax.ShapeDtypeStruct((ROWS, CHUNK), SENT)
    joined, edge, relay = pl.pallas_call(
        far_kernel,
        out_shape=[
            jax.ShapeDtypeStruct((ROWS * M, KX), jnp.bfloat16),
            jax.ShapeDtypeStruct((ROWS * M, 256), jnp.float32),
            sent,
        ],
        in_specs=whole(12),
        out_specs=whole(3),
        compiler_params=pltpu.CompilerParams(vmem_limit_bytes=SCRATCH),
        cost_estimate=pl.CostEstimate(flops=3 << 30, bytes_accessed=8 << 20, transcendentals=0),
        name="far_kernel",
    )(scale, got, fields, table_x, *order_tables(), last)
    relay = ahead(relay, 1)
    direct, mirrored = pl.pallas_call(
        near_kernel,
        out_shape=[sent, piece],
        in_specs=whole(6),
        out_specs=whole(2),
        compiler_params=pltpu.CompilerParams(vmem_limit_bytes=SCRATCH),
        cost_estimate=pl.CostEstimate(flops=NEAR_FLOPS, bytes_accessed=4 << 20, transcendentals=0),
        name="near_kernel",
    )(scale, joined, edge, fields, table_x, last)
    direct = ahead(direct, 1)
    passed = (mirrored + relay.astype(jnp.float32)).astype(SENT)
    passed, joined = lax.optimization_barrier((passed, joined))
    across = ahead(passed, 3)
    own = pl.pallas_call(
        own_field_kernel,
        out_shape=piece,
        in_specs=whole(6),
        out_specs=pl.BlockSpec(memory_space=pltpu.VMEM),
        compiler_params=pltpu.CompilerParams(vmem_limit_bytes=SCRATCH),
        cost_estimate=pl.CostEstimate(flops=NEAR_FLOPS, bytes_accessed=4 << 20, transcendentals=0),
        name="own_field_kernel",
    )(scale, joined, edge, fields, table_x, last)
    return (own + direct.astype(jnp.float32)) + across.astype(jnp.float32)


def ahead(piece, step):
    return lax.ppermute(piece, "band", [(i, i ^ step) for i in range(BANDS)])


def solution(mesh):
    placed = (P("band", None, ("gx", "gy"), None), P("band", None, "gx", "gy", None), P())
    return jax.shard_map(
        body, mesh=mesh, in_specs=placed, out_specs=P(("gx", "gy"), "band"), check_vma=False
    )
```

```python
import functools
import math

import jax
import jax.numpy as jnp
import ml_dtypes
import numpy as np
from jax import lax
from jax.experimental import pallas as pl
from jax.experimental.pallas import tpu as pltpu
from jax.sharding import PartitionSpec as P

NX = 2560
NY = 1408
KX = 1024
KY = 256
M = 16
BANDS = 4
GX = 16
GY = 4
DESTS = GX * GY
ROWS = NY // DESTS
PAD = 24
WAVES = KX // GX
HALF = WAVES // 2
MEMBERS = M // GY
CHUNK = NX // BANDS
SENT = jnp.bfloat16
SCRATCH = 16 * 1024 * 1024
OWN_FLOPS = 10 ** 10
NEAR_FLOPS = 10 ** 10
ROWS_FLOPS = 2 * 10 ** 10


def low(array):
    return np.asarray(array, dtype=np.float64).astype(ml_dtypes.bfloat16)


def trig(wave, position, period):
    angle = np.mod(np.multiply.outer(wave, position), period) * (2.0 * math.pi / period)
    return np.cos(angle), np.sin(angle)


def first_wave(block):
    return WAVES * (block - GX // 2) if block >= GX // 2 else WAVES * (GX // 2 - 1 - block) + HALF


@functools.lru_cache(None)
def fold_tables():
    fold = np.zeros((2, 2, MEMBERS, HALF, (WAVES + HALF) * MEMBERS))
    for member in range(MEMBERS):
        for pair in range(HALF):
            own = MEMBERS * pair + member
            for part, sign in ((0, 1.0), (1, -1.0)):
                fold[0, part, member, pair, own] = 1.0
                if pair > 0:
                    fold[0, part, member, pair, MEMBERS * (WAVES + HALF - pair) + member] = sign
                fold[1, part, member, pair, MEMBERS * WAVES + own] = 1.0
                fold[1, part, member, pair, MEMBERS * (HALF - pair) + member] = sign
    return low(fold.reshape(2, 2 * MEMBERS * HALF, (WAVES + HALF) * MEMBERS))


@functools.lru_cache(None)
def row_tables():
    cosine, sine = trig(np.arange(NY), np.arange(KY), NY)
    table = np.zeros((DESTS, PAD, 2 * KY))
    table[:, :ROWS] = np.concatenate([cosine, sine], axis=1).reshape(DESTS, ROWS, 2 * KY)
    coarse = np.concatenate(trig(np.arange(DESTS) * ROWS, np.arange(KY), NY), axis=1)
    fine = np.stack(trig(np.arange(32), np.arange(KY), NY)).astype(np.float32)
    return low(table.reshape(DESTS * PAD, 2 * KY)), low(coarse), fine


@functools.lru_cache(None)
def column_tables():
    waves = np.concatenate([first_wave(block) + np.arange(HALF) for block in range(GX)])
    columns = np.arange(NX)
    cosine, sine = trig(waves, columns, NX)
    last = np.zeros((8, columns.size))
    last[0], last[1] = trig(np.array([KX // 2]), columns, NX)
    return low(np.concatenate([cosine, -sine])), low(last).astype(np.float32)


@functools.lru_cache(None)
def order_tables():
    row_order = np.zeros((ROWS, GY, MEMBERS, MEMBERS, GY, PAD))
    pick = np.zeros((ROWS, GY, MEMBERS, 2, MEMBERS, 32))
    same = np.zeros((ROWS, GY, MEMBERS, 128))
    for row in range(ROWS):
        for column in range(GY):
            for member in range(MEMBERS):
                row_order[row, column, member, member, column, row] = 1.0
                pick[row, column, member, :, member, row] = 1.0
                same[row, column, member, column:64:GY] = 1.0
    gather = np.zeros((128, GX // 2, GY, PAD))
    lane_part = np.zeros((128, 256))
    join = np.zeros((128, KX))
    spread = np.zeros((128, 256))
    for slot in range(64):
        part, block, column = slot // 32, slot % 32 // GY, slot % GY
        gather[slot, block, column, ROWS] = 1.0
        lane_part[slot, part * 128 : part * 128 + 128] = 1.0
        if block == 0:
            spread[slot, part * 128 : part * 128 + 128] = 1.0
        else:
            other = GX - block
            join[slot, part * 512 + other * 32] = 1.0 - 2.0 * part
    return (
        low(row_order.reshape(ROWS * M, MEMBERS * GY * PAD)),
        low(pick.reshape(ROWS * M, 256)),
        same.reshape(ROWS * M, 128).astype(np.float32),
        low(gather.reshape(128, DESTS // 2 * PAD)),
        lane_part.astype(np.float32),
        low(join),
        low(spread),
    )


def nn(a, b):
    return jnp.dot(a, b, preferred_element_type=jnp.float32)


def nt(a, b):
    return lax.dot_general(a, b, (((1,), (1,)), ((), ())), preferred_element_type=jnp.float32)


def place(block, rows):
    negative = (block < GX // 2).astype(jnp.int32)
    return negative, jnp.where(negative == 1, WAVES * (GX // 2 - 1 - block), WAVES * (block - GX // 2))


def pair_mask(base, negative, cut):
    shape = (2 * MEMBERS * HALF, KY)
    wave = base + HALF * negative + (lax.broadcasted_iota(jnp.int32, shape, 0) & (HALF - 1))
    wave_y = lax.broadcasted_iota(jnp.int32, shape, 1)
    return wave * wave + wave_y * wave_y < cut


def own_kernel(cut_ref, own_ref, fold_ref, coarse_ref, fine_ref, folded_ref, extra_ref, scale_ref):
    block = lax.axis_index("gx")
    cut = cut_ref[lax.axis_index("band")]
    negative, base = place(block, WAVES)
    fold = fold_ref[negative, :, : WAVES * MEMBERS]
    inside = pair_mask(base, negative, cut)
    for part in range(2):
        folded_ref[part] = jnp.where(inside, nn(fold, own_ref[part]), 0.0)

    wave_y = lax.broadcasted_iota(jnp.int32, (MEMBERS, KY), 1)
    last = base + WAVES
    edge = last * last + wave_y * wave_y < cut
    edge_real = jnp.where(edge, own_ref[0, :16].astype(jnp.float32)[:MEMBERS], 0.0)
    edge_imag = jnp.where(edge, own_ref[1, :16].astype(jnp.float32)[:MEMBERS], 0.0)
    cosine, sine = fine_ref[0], fine_ref[1]
    even = jnp.concatenate(
        [edge_real[m : m + 1] * cosine - edge_imag[m : m + 1] * sine for m in range(MEMBERS)], axis=0
    )
    odd = jnp.concatenate(
        [edge_real[m : m + 1] * sine + edge_imag[m : m + 1] * cosine for m in range(MEMBERS)], axis=0
    )
    turned = jnp.concatenate(
        [jnp.concatenate([even, -odd], axis=1), jnp.concatenate([odd, even], axis=1)], axis=0
    ).astype(jnp.bfloat16)
    extra_ref[...] = nt(coarse_ref[...], turned)

    shape = (KX, KY)
    wave_x = lax.broadcasted_iota(jnp.int32, shape, 0) - KX // 2
    wave_y = lax.broadcasted_iota(jnp.int32, shape, 1)
    inside = (wave_x * wave_x + wave_y * wave_y < cut).astype(jnp.float32)
    count = jnp.sum(jnp.sum(inside.reshape(KX // 8, 8, KY), axis=0))
    scale_ref[...] = lax.rsqrt(jnp.full((8, 128), count)) * (1.0 / math.sqrt(M * BANDS))


def rows_kernel(cut_ref, folded_ref, extra_ref, mirror_ref, fold_ref, table_ref, out_ref):
    cut = cut_ref[lax.axis_index("band")]
    negative, base = place(lax.axis_index("gx"), WAVES)
    fold = fold_ref[negative, :, WAVES * MEMBERS :]
    inside = pair_mask(base, negative, cut)
    real = folded_ref[0] + jnp.where(inside, nn(fold, mirror_ref[0]), 0.0)
    imag = folded_ref[1] + jnp.where(inside, nn(fold, mirror_ref[1]), 0.0)
    half = MEMBERS * HALF
    with_cosine = jnp.concatenate([real[:half], imag[half:]], axis=0)
    with_sine = jnp.concatenate([-imag[:half], real[half:]], axis=0)
    weights = jnp.concatenate([with_cosine, with_sine], axis=1).astype(jnp.bfloat16)
    dests = DESTS // 4
    row = lax.broadcasted_iota(jnp.int32, (dests, PAD, 256), 1)
    for part in range(4):
        rows = pl.ds(part * dests * PAD, dests * PAD)
        block = nt(table_ref[rows, :], weights).reshape(dests, PAD, 256)
        extra = extra_ref[part * dests : (part + 1) * dests, :].reshape(dests, 1, 256)
        out_ref[rows, :] = jnp.where(row == ROWS, extra, block).reshape(dests * PAD, 256).astype(jnp.bfloat16)


def weigh(alpha, edge, last_ref, start, ensemble_ref, chunk, scale_ref):
    columns = pl.ds(pl.multiple_of(start, CHUNK), CHUNK)
    repeat = CHUNK // 128
    cosine, sine = last_ref[:1, columns], last_ref[1:2, columns]
    alpha = alpha + jnp.concatenate([edge[:, :128]] * repeat, axis=1) * cosine
    alpha = alpha + jnp.concatenate([edge[:, 128:]] * repeat, axis=1) * sine
    fields = ensemble_ref[:, :, pl.ds(pl.multiple_of(chunk * CHUNK, CHUNK), CHUNK)].astype(jnp.float32)
    return jnp.sum(alpha.reshape(ROWS, M, CHUNK) * fields, axis=1) * scale_ref[:1, :1]


def far_kernel(
    scale_ref,
    got_ref,
    ensemble_ref,
    table_ref,
    row_ref,
    pick_ref,
    same_ref,
    gather_ref,
    part_ref,
    join_ref,
    spread_ref,
    last_ref,
    joined_ref,
    edge_ref,
    relay_ref,
):
    span = GY * PAD
    members = []
    for m in range(MEMBERS):
        pieces = []
        for part in range(2):
            lane = part * 128 + m * HALF
            pieces += [got_ref[block * span : (block + 1) * span, lane : lane + HALF] for block in range(GX)]
        members.append(jnp.concatenate(pieces, axis=1))
    edge = nn(
        gather_ref[...],
        got_ref[: GX // 2 * GY * PAD, :],
    )
    edge = (nt(pick_ref[...], (edge * part_ref[...]).astype(jnp.bfloat16)) * same_ref[...]).astype(jnp.bfloat16)
    joined = nn(
        jnp.concatenate([row_ref[...], edge], axis=1), jnp.concatenate(members + [join_ref[...]], axis=0)
    ).astype(jnp.bfloat16)
    joined_ref[...] = joined
    edge = nn(edge, spread_ref[...])
    edge_ref[...] = edge
    chunk = BANDS - 1 - (lax.axis_index("band") ^ 1)
    start = pl.multiple_of(chunk * CHUNK, CHUNK)
    alpha = nn(joined, table_ref[:, pl.ds(start, CHUNK)])
    relay_ref[...] = weigh(alpha, edge, last_ref, start, ensemble_ref, chunk, scale_ref).astype(relay_ref.dtype)


def chunk_field(chunk, joined, edge, last_ref, ensemble_ref, table_ref, scale_ref):
    start = pl.multiple_of(chunk * CHUNK, CHUNK)
    alpha = nn(joined, table_ref[:, pl.ds(start, CHUNK)])
    return weigh(alpha, edge, last_ref, start, ensemble_ref, chunk, scale_ref)


def near_kernel(scale_ref, joined_ref, edge_ref, ensemble_ref, table_ref, last_ref, direct_ref, mirrored_ref):
    band = lax.axis_index("band")
    refs = (last_ref, ensemble_ref, table_ref, scale_ref)
    joined, edge = joined_ref[...], edge_ref[...]
    mirrored_ref[...] = chunk_field(BANDS - 1 - band, joined, edge, *refs)
    direct_ref[...] = chunk_field(band ^ 1, joined, edge, *refs).astype(direct_ref.dtype)


def own_field_kernel(scale_ref, joined_ref, edge_ref, ensemble_ref, table_ref, last_ref, own_ref):
    band = lax.axis_index("band")
    own_ref[...] = chunk_field(
        band, joined_ref[...], edge_ref[...], last_ref, ensemble_ref, table_ref, scale_ref
    )


def whole(count):
    return [pl.BlockSpec(memory_space=pltpu.VMEM) for _ in range(count)]


def body(ensemble, spectral, band_cut):
    own = spectral[0].reshape(2, WAVES * MEMBERS, KY)
    mirror = lax.ppermute(own[:, HALF * MEMBERS :], "gx", [(i, GX - 1 - i) for i in range(GX)])
    table_y, coarse, fine = row_tables()
    smem = pl.BlockSpec(memory_space=pltpu.SMEM)
    folded, extra, scale = pl.pallas_call(
        own_kernel,
        out_shape=[
            jax.ShapeDtypeStruct((2, 256, KY), jnp.float32),
            jax.ShapeDtypeStruct((DESTS, 256), jnp.float32),
            jax.ShapeDtypeStruct((8, 128), jnp.float32),
        ],
        in_specs=[smem] + whole(4),
        out_specs=whole(3),
        compiler_params=pltpu.CompilerParams(vmem_limit_bytes=SCRATCH),
        cost_estimate=pl.CostEstimate(flops=OWN_FLOPS, bytes_accessed=1 << 20, transcendentals=0),
        name="own_kernel",
    )(band_cut, own, fold_tables(), coarse, fine)
    rows = pl.pallas_call(
        rows_kernel,
        out_shape=jax.ShapeDtypeStruct((DESTS * PAD, 256), jnp.bfloat16),
        in_specs=[smem] + whole(5),
        out_specs=pl.BlockSpec(memory_space=pltpu.VMEM),
        compiler_params=pltpu.CompilerParams(vmem_limit_bytes=SCRATCH),
        cost_estimate=pl.CostEstimate(flops=ROWS_FLOPS, bytes_accessed=4 << 20, transcendentals=0),
        name="rows_kernel",
    )(band_cut, folded, extra, mirror, fold_tables(), table_y)
    got = lax.all_to_all(rows, ("gx", "gy"), split_axis=0, concat_axis=0, tiled=True)
    fields, (table_x, last) = ensemble[0].transpose(1, 0, 2), column_tables()
    piece = jax.ShapeDtypeStruct((ROWS, CHUNK), jnp.float32)
    sent = jax.ShapeDtypeStruct((ROWS, CHUNK), SENT)
    joined, edge, relay = pl.pallas_call(
        far_kernel,
        out_shape=[
            jax.ShapeDtypeStruct((ROWS * M, KX), jnp.bfloat16),
            jax.ShapeDtypeStruct((ROWS * M, 256), jnp.float32),
            sent,
        ],
        in_specs=whole(12),
        out_specs=whole(3),
        compiler_params=pltpu.CompilerParams(vmem_limit_bytes=SCRATCH),
        cost_estimate=pl.CostEstimate(flops=3 << 30, bytes_accessed=8 << 20, transcendentals=0),
        name="far_kernel",
    )(scale, got, fields, table_x, *order_tables(), last)
    relay = ahead(relay, 1)
    direct, mirrored = pl.pallas_call(
        near_kernel,
        out_shape=[sent, piece],
        in_specs=whole(6),
        out_specs=whole(2),
        compiler_params=pltpu.CompilerParams(vmem_limit_bytes=SCRATCH),
        cost_estimate=pl.CostEstimate(flops=NEAR_FLOPS, bytes_accessed=4 << 20, transcendentals=0),
        name="near_kernel",
    )(scale, joined, edge, fields, table_x, last)
    direct = ahead(direct, 1)
    passed = (mirrored + relay.astype(jnp.float32)).astype(SENT)
    passed, joined = lax.optimization_barrier((passed, joined))
    across = ahead(passed, 3)
    own = pl.pallas_call(
        own_field_kernel,
        out_shape=piece,
        in_specs=whole(6),
        out_specs=pl.BlockSpec(memory_space=pltpu.VMEM),
        compiler_params=pltpu.CompilerParams(vmem_limit_bytes=SCRATCH),
        cost_estimate=pl.CostEstimate(flops=NEAR_FLOPS, bytes_accessed=4 << 20, transcendentals=0),
        name="own_field_kernel",
    )(scale, joined, edge, fields, table_x, last)
    return (own + direct.astype(jnp.float32)) + across.astype(jnp.float32)


def ahead(piece, step):
    return lax.ppermute(piece, "band", [(i, i ^ step) for i in range(BANDS)])


def solution(mesh):
    placed = (P("band", None, ("gx", "gy"), None), P("band", None, "gx", "gy", None), P())
    return jax.shard_map(
        body, mesh=mesh, in_specs=placed, out_specs=P(("gx", "gy"), "band"), check_vma=False
    )
```

```python
import functools
import math

import jax
import jax.numpy as jnp
import ml_dtypes
import numpy as np
from jax import lax
from jax.experimental import pallas as pl
from jax.experimental.pallas import tpu as pltpu
from jax.sharding import PartitionSpec as P

NX = 2560
NY = 1408
KX = 1024
KY = 256
M = 16
BANDS = 4
GX = 16
GY = 4
DESTS = GX * GY
ROWS = NY // DESTS
PAD = 24
WAVES = KX // GX
HALF = WAVES // 2
MEMBERS = M // GY
CHUNK = NX // BANDS
SENT = jnp.bfloat16
SCRATCH = 16 * 1024 * 1024
OWN_FLOPS = 10 ** 10
NEAR_FLOPS = 10 ** 10
ROWS_FLOPS = 2 * 10 ** 10


def low(array):
    return np.asarray(array, dtype=np.float64).astype(ml_dtypes.bfloat16)


def trig(wave, position, period):
    angle = np.mod(np.multiply.outer(wave, position), period) * (2.0 * math.pi / period)
    return np.cos(angle), np.sin(angle)


def first_wave(block):
    return WAVES * (block - GX // 2) if block >= GX // 2 else WAVES * (GX // 2 - 1 - block) + HALF


@functools.lru_cache(None)
def fold_tables():
    fold = np.zeros((2, 2, MEMBERS, HALF, (WAVES + HALF) * MEMBERS))
    for member in range(MEMBERS):
        for pair in range(HALF):
            own = MEMBERS * pair + member
            for part, sign in ((0, 1.0), (1, -1.0)):
                fold[0, part, member, pair, own] = 1.0
                if pair > 0:
                    fold[0, part, member, pair, MEMBERS * (WAVES + HALF - pair) + member] = sign
                fold[1, part, member, pair, MEMBERS * WAVES + own] = 1.0
                fold[1, part, member, pair, MEMBERS * (HALF - pair) + member] = sign
    return low(fold.reshape(2, 2 * MEMBERS * HALF, (WAVES + HALF) * MEMBERS))


@functools.lru_cache(None)
def row_tables():
    cosine, sine = trig(np.arange(NY), np.arange(KY), NY)
    table = np.zeros((DESTS, PAD, 2 * KY))
    table[:, :ROWS] = np.concatenate([cosine, sine], axis=1).reshape(DESTS, ROWS, 2 * KY)
    coarse = np.concatenate(trig(np.arange(DESTS) * ROWS, np.arange(KY), NY), axis=1)
    fine = np.stack(trig(np.arange(32), np.arange(KY), NY)).astype(np.float32)
    return low(table.reshape(DESTS * PAD, 2 * KY)), low(coarse), fine


@functools.lru_cache(None)
def column_tables():
    waves = np.concatenate([first_wave(block) + np.arange(HALF) for block in range(GX)])
    columns = np.arange(NX)
    cosine, sine = trig(waves, columns, NX)
    last = np.zeros((8, columns.size))
    last[0], last[1] = trig(np.array([KX // 2]), columns, NX)
    return low(np.concatenate([cosine, -sine])), low(last).astype(np.float32)


@functools.lru_cache(None)
def order_tables():
    row_order = np.zeros((ROWS, GY, MEMBERS, MEMBERS, GY, PAD))
    pick = np.zeros((ROWS, GY, MEMBERS, 2, MEMBERS, 32))
    same = np.zeros((ROWS, GY, MEMBERS, 128))
    for row in range(ROWS):
        for column in range(GY):
            for member in range(MEMBERS):
                row_order[row, column, member, member, column, row] = 1.0
                pick[row, column, member, :, member, row] = 1.0
                same[row, column, member, column:64:GY] = 1.0
    gather = np.zeros((128, GX // 2, GY, PAD))
    lane_part = np.zeros((128, 256))
    join = np.zeros((128, KX))
    spread = np.zeros((128, 256))
    for slot in range(64):
        part, block, column = slot // 32, slot % 32 // GY, slot % GY
        gather[slot, block, column, ROWS] = 1.0
        lane_part[slot, part * 128 : part * 128 + 128] = 1.0
        if block == 0:
            spread[slot, part * 128 : part * 128 + 128] = 1.0
        else:
            other = GX - block
            join[slot, part * 512 + other * 32] = 1.0 - 2.0 * part
    return (
        low(row_order.reshape(ROWS * M, MEMBERS * GY * PAD)),
        low(pick.reshape(ROWS * M, 256)),
        same.reshape(ROWS * M, 128).astype(np.float32),
        low(gather.reshape(128, DESTS // 2 * PAD)),
        lane_part.astype(np.float32),
        low(join),
        low(spread),
    )


def nn(a, b):
    return jnp.dot(a, b, preferred_element_type=jnp.float32)


def nt(a, b):
    return lax.dot_general(a, b, (((1,), (1,)), ((), ())), preferred_element_type=jnp.float32)


def place(block, rows):
    negative = (block < GX // 2).astype(jnp.int32)
    return negative, jnp.where(negative == 1, WAVES * (GX // 2 - 1 - block), WAVES * (block - GX // 2))


def pair_mask(base, negative, cut):
    shape = (2 * MEMBERS * HALF, KY)
    wave = base + HALF * negative + (lax.broadcasted_iota(jnp.int32, shape, 0) & (HALF - 1))
    wave_y = lax.broadcasted_iota(jnp.int32, shape, 1)
    return wave * wave + wave_y * wave_y < cut


def own_kernel(cut_ref, own_ref, fold_ref, coarse_ref, fine_ref, folded_ref, extra_ref, scale_ref):
    block = lax.axis_index("gx")
    cut = cut_ref[lax.axis_index("band")]
    negative, base = place(block, WAVES)
    fold = fold_ref[negative, :, : WAVES * MEMBERS]
    inside = pair_mask(base, negative, cut)
    for part in range(2):
        folded_ref[part] = jnp.where(inside, nn(fold, own_ref[part]), 0.0)

    wave_y = lax.broadcasted_iota(jnp.int32, (MEMBERS, KY), 1)
    last = base + WAVES
    edge = last * last + wave_y * wave_y < cut
    edge_real = jnp.where(edge, own_ref[0, :16].astype(jnp.float32)[:MEMBERS], 0.0)
    edge_imag = jnp.where(edge, own_ref[1, :16].astype(jnp.float32)[:MEMBERS], 0.0)
    cosine, sine = fine_ref[0], fine_ref[1]
    even = jnp.concatenate(
        [edge_real[m : m + 1] * cosine - edge_imag[m : m + 1] * sine for m in range(MEMBERS)], axis=0
    )
    odd = jnp.concatenate(
        [edge_real[m : m + 1] * sine + edge_imag[m : m + 1] * cosine for m in range(MEMBERS)], axis=0
    )
    turned = jnp.concatenate(
        [jnp.concatenate([even, -odd], axis=1), jnp.concatenate([odd, even], axis=1)], axis=0
    ).astype(jnp.bfloat16)
    extra_ref[...] = nt(coarse_ref[...], turned)

    shape = (KX, KY)
    wave_x = lax.broadcasted_iota(jnp.int32, shape, 0) - KX // 2
    wave_y = lax.broadcasted_iota(jnp.int32, shape, 1)
    inside = (wave_x * wave_x + wave_y * wave_y < cut).astype(jnp.float32)
    count = jnp.sum(jnp.sum(inside.reshape(KX // 8, 8, KY), axis=0))
    scale_ref[...] = lax.rsqrt(jnp.full((8, 128), count)) * (1.0 / math.sqrt(M * BANDS))


def rows_kernel(cut_ref, folded_ref, extra_ref, mirror_ref, fold_ref, table_ref, out_ref):
    cut = cut_ref[lax.axis_index("band")]
    negative, base = place(lax.axis_index("gx"), WAVES)
    fold = fold_ref[negative, :, WAVES * MEMBERS :]
    inside = pair_mask(base, negative, cut)
    real = folded_ref[0] + jnp.where(inside, nn(fold, mirror_ref[0]), 0.0)
    imag = folded_ref[1] + jnp.where(inside, nn(fold, mirror_ref[1]), 0.0)
    half = MEMBERS * HALF
    with_cosine = jnp.concatenate([real[:half], imag[half:]], axis=0)
    with_sine = jnp.concatenate([-imag[:half], real[half:]], axis=0)
    weights = jnp.concatenate([with_cosine, with_sine], axis=1).astype(jnp.bfloat16)
    dests = DESTS // 2
    row = lax.broadcasted_iota(jnp.int32, (dests, PAD, 256), 1)
    for part in range(2):
        rows = pl.ds(part * dests * PAD, dests * PAD)
        block = nt(table_ref[rows, :], weights).reshape(dests, PAD, 256)
        extra = extra_ref[part * dests : (part + 1) * dests, :].reshape(dests, 1, 256)
        out_ref[rows, :] = jnp.where(row == ROWS, extra, block).reshape(dests * PAD, 256).astype(jnp.bfloat16)


def weigh(alpha, edge, last_ref, start, ensemble_ref, chunk, scale_ref):
    columns = pl.ds(pl.multiple_of(start, CHUNK), CHUNK)
    repeat = CHUNK // 128
    cosine, sine = last_ref[:1, columns], last_ref[1:2, columns]
    alpha = alpha + jnp.concatenate([edge[:, :128]] * repeat, axis=1) * cosine
    alpha = alpha + jnp.concatenate([edge[:, 128:]] * repeat, axis=1) * sine
    fields = ensemble_ref[:, :, pl.ds(pl.multiple_of(chunk * CHUNK, CHUNK), CHUNK)].astype(jnp.float32)
    return jnp.sum(alpha.reshape(ROWS, M, CHUNK) * fields, axis=1) * scale_ref[:1, :1]


def far_kernel(
    scale_ref,
    got_ref,
    ensemble_ref,
    table_ref,
    row_ref,
    pick_ref,
    same_ref,
    gather_ref,
    part_ref,
    join_ref,
    spread_ref,
    last_ref,
    joined_ref,
    edge_ref,
    relay_ref,
):
    span = GY * PAD
    members = []
    for m in range(MEMBERS):
        pieces = []
        for part in range(2):
            lane = part * 128 + m * HALF
            pieces += [got_ref[block * span : (block + 1) * span, lane : lane + HALF] for block in range(GX)]
        members.append(jnp.concatenate(pieces, axis=1))
    edge = nn(
        gather_ref[...],
        got_ref[: GX // 2 * GY * PAD, :],
    )
    edge = (nt(pick_ref[...], (edge * part_ref[...]).astype(jnp.bfloat16)) * same_ref[...]).astype(jnp.bfloat16)
    joined = nn(
        jnp.concatenate([row_ref[...], edge], axis=1), jnp.concatenate(members + [join_ref[...]], axis=0)
    ).astype(jnp.bfloat16)
    joined_ref[...] = joined
    edge = nn(edge, spread_ref[...])
    edge_ref[...] = edge.astype(jnp.bfloat16)
    chunk = BANDS - 1 - (lax.axis_index("band") ^ 1)
    start = pl.multiple_of(chunk * CHUNK, CHUNK)
    alpha = nn(joined, table_ref[:, pl.ds(start, CHUNK)])
    relay_ref[...] = weigh(alpha, edge, last_ref, start, ensemble_ref, chunk, scale_ref).astype(relay_ref.dtype)


def chunk_field(chunk, joined, edge, last_ref, ensemble_ref, table_ref, scale_ref):
    start = pl.multiple_of(chunk * CHUNK, CHUNK)
    alpha = nn(joined, table_ref[:, pl.ds(start, CHUNK)])
    return weigh(alpha, edge, last_ref, start, ensemble_ref, chunk, scale_ref)


def near_kernel(scale_ref, joined_ref, edge_ref, ensemble_ref, table_ref, last_ref, direct_ref, mirrored_ref):
    band = lax.axis_index("band")
    refs = (last_ref, ensemble_ref, table_ref, scale_ref)
    joined, edge = joined_ref[...], edge_ref[...].astype(jnp.float32)
    mirrored_ref[...] = chunk_field(BANDS - 1 - band, joined, edge, *refs)
    direct_ref[...] = chunk_field(band ^ 1, joined, edge, *refs).astype(direct_ref.dtype)


def own_field_kernel(scale_ref, joined_ref, edge_ref, ensemble_ref, table_ref, last_ref, own_ref):
    band = lax.axis_index("band")
    own_ref[...] = chunk_field(
        band, joined_ref[...], edge_ref[...].astype(jnp.float32), last_ref, ensemble_ref, table_ref, scale_ref
    )


def whole(count):
    return [pl.BlockSpec(memory_space=pltpu.VMEM) for _ in range(count)]


def body(ensemble, spectral, band_cut):
    own = spectral[0].reshape(2, WAVES * MEMBERS, KY)
    mirror = lax.ppermute(own[:, HALF * MEMBERS :], "gx", [(i, GX - 1 - i) for i in range(GX)])
    table_y, coarse, fine = row_tables()
    smem = pl.BlockSpec(memory_space=pltpu.SMEM)
    folded, extra, scale = pl.pallas_call(
        own_kernel,
        out_shape=[
            jax.ShapeDtypeStruct((2, 256, KY), jnp.float32),
            jax.ShapeDtypeStruct((DESTS, 256), jnp.float32),
            jax.ShapeDtypeStruct((8, 128), jnp.float32),
        ],
        in_specs=[smem] + whole(4),
        out_specs=whole(3),
        compiler_params=pltpu.CompilerParams(vmem_limit_bytes=SCRATCH),
        cost_estimate=pl.CostEstimate(flops=OWN_FLOPS, bytes_accessed=1 << 20, transcendentals=0),
        name="own_kernel",
    )(band_cut, own, fold_tables(), coarse, fine)
    rows = pl.pallas_call(
        rows_kernel,
        out_shape=jax.ShapeDtypeStruct((DESTS * PAD, 256), jnp.bfloat16),
        in_specs=[smem] + whole(5),
        out_specs=pl.BlockSpec(memory_space=pltpu.VMEM),
        compiler_params=pltpu.CompilerParams(vmem_limit_bytes=SCRATCH),
        cost_estimate=pl.CostEstimate(flops=ROWS_FLOPS, bytes_accessed=4 << 20, transcendentals=0),
        name="rows_kernel",
    )(band_cut, folded, extra, mirror, fold_tables(), table_y)
    got = lax.all_to_all(rows, ("gx", "gy"), split_axis=0, concat_axis=0, tiled=True)
    fields, (table_x, last) = ensemble[0].transpose(1, 0, 2), column_tables()
    piece = jax.ShapeDtypeStruct((ROWS, CHUNK), jnp.float32)
    sent = jax.ShapeDtypeStruct((ROWS, CHUNK), SENT)
    joined, edge, relay = pl.pallas_call(
        far_kernel,
        out_shape=[
            jax.ShapeDtypeStruct((ROWS * M, KX), jnp.bfloat16),
            jax.ShapeDtypeStruct((ROWS * M, 256), jnp.bfloat16),
            sent,
        ],
        in_specs=whole(12),
        out_specs=whole(3),
        compiler_params=pltpu.CompilerParams(vmem_limit_bytes=SCRATCH),
        cost_estimate=pl.CostEstimate(flops=3 << 30, bytes_accessed=8 << 20, transcendentals=0),
        name="far_kernel",
    )(scale, got, fields, table_x, *order_tables(), last)
    relay = ahead(relay, 1)
    direct, mirrored = pl.pallas_call(
        near_kernel,
        out_shape=[sent, piece],
        in_specs=whole(6),
        out_specs=whole(2),
        compiler_params=pltpu.CompilerParams(vmem_limit_bytes=SCRATCH),
        cost_estimate=pl.CostEstimate(flops=NEAR_FLOPS, bytes_accessed=4 << 20, transcendentals=0),
        name="near_kernel",
    )(scale, joined, edge, fields, table_x, last)
    direct = ahead(direct, 1)
    passed = (mirrored + relay.astype(jnp.float32)).astype(SENT)
    passed, joined = lax.optimization_barrier((passed, joined))
    across = ahead(passed, 3)
    own = pl.pallas_call(
        own_field_kernel,
        out_shape=piece,
        in_specs=whole(6),
        out_specs=pl.BlockSpec(memory_space=pltpu.VMEM),
        compiler_params=pltpu.CompilerParams(vmem_limit_bytes=SCRATCH),
        cost_estimate=pl.CostEstimate(flops=NEAR_FLOPS, bytes_accessed=4 << 20, transcendentals=0),
        name="own_field_kernel",
    )(scale, joined, edge, fields, table_x, last)
    return (own + direct.astype(jnp.float32)) + across.astype(jnp.float32)


def ahead(piece, step):
    return lax.ppermute(piece, "band", [(i, i ^ step) for i in range(BANDS)])


def solution(mesh):
    placed = (P("band", None, ("gx", "gy"), None), P("band", None, "gx", "gy", None), P())
    return jax.shard_map(
        body, mesh=mesh, in_specs=placed, out_specs=P(("gx", "gy"), "band"), check_vma=False
    )
```

```python
import functools
import math

import jax
import jax.numpy as jnp
import ml_dtypes
import numpy as np
from jax import lax
from jax.experimental import pallas as pl
from jax.experimental.pallas import tpu as pltpu
from jax.sharding import PartitionSpec as P

NX = 2560
NY = 1408
KX = 1024
KY = 256
M = 16
BANDS = 4
GX = 16
GY = 4
DESTS = GX * GY
ROWS = NY // DESTS
PAD = 24
WAVES = KX // GX
HALF = WAVES // 2
MEMBERS = M // GY
CHUNK = NX // BANDS
SENT = jnp.bfloat16
SCRATCH = 16 * 1024 * 1024
OWN_FLOPS = 10 ** 10
NEAR_FLOPS = 10 ** 10
ROWS_FLOPS = 2 * 10 ** 10


def low(array):
    return np.asarray(array, dtype=np.float64).astype(ml_dtypes.bfloat16)


def trig(wave, position, period):
    angle = np.mod(np.multiply.outer(wave, position), period) * (2.0 * math.pi / period)
    return np.cos(angle), np.sin(angle)


def first_wave(block):
    return WAVES * (block - GX // 2) if block >= GX // 2 else WAVES * (GX // 2 - 1 - block) + HALF


@functools.lru_cache(None)
def fold_tables():
    fold = np.zeros((2, 2, MEMBERS, HALF, (WAVES + HALF) * MEMBERS))
    for member in range(MEMBERS):
        for pair in range(HALF):
            own = MEMBERS * pair + member
            for part, sign in ((0, 1.0), (1, -1.0)):
                fold[0, part, member, pair, own] = 1.0
                if pair > 0:
                    fold[0, part, member, pair, MEMBERS * (WAVES + HALF - pair) + member] = sign
                fold[1, part, member, pair, MEMBERS * WAVES + own] = 1.0
                fold[1, part, member, pair, MEMBERS * (HALF - pair) + member] = sign
    return low(fold.reshape(2, 2 * MEMBERS * HALF, (WAVES + HALF) * MEMBERS))


@functools.lru_cache(None)
def row_tables():
    cosine, sine = trig(np.arange(NY), np.arange(KY), NY)
    table = np.zeros((DESTS, PAD, 2 * KY))
    table[:, :ROWS] = np.concatenate([cosine, sine], axis=1).reshape(DESTS, ROWS, 2 * KY)
    coarse = np.concatenate(trig(np.arange(DESTS) * ROWS, np.arange(KY), NY), axis=1)
    fine = np.stack(trig(np.arange(32), np.arange(KY), NY)).astype(np.float32)
    return low(table.reshape(DESTS * PAD, 2 * KY)), low(coarse), fine


@functools.lru_cache(None)
def column_tables():
    waves = np.concatenate([first_wave(block) + np.arange(HALF) for block in range(GX)])
    columns = np.arange(NX)
    cosine, sine = trig(waves, columns, NX)
    last = np.zeros((8, columns.size))
    last[0], last[1] = trig(np.array([KX // 2]), columns, NX)
    return low(np.concatenate([cosine, -sine])), low(last).astype(np.float32)


@functools.lru_cache(None)
def order_tables():
    row_order = np.zeros((ROWS, GY, MEMBERS, MEMBERS, GY, PAD))
    pick = np.zeros((ROWS, GY, MEMBERS, 2, MEMBERS, 32))
    same = np.zeros((ROWS, GY, MEMBERS, 128))
    for row in range(ROWS):
        for column in range(GY):
            for member in range(MEMBERS):
                row_order[row, column, member, member, column, row] = 1.0
                pick[row, column, member, :, member, row] = 1.0
                same[row, column, member, column:64:GY] = 1.0
    gather = np.zeros((128, GX // 2, GY, PAD))
    lane_part = np.zeros((128, 256))
    join = np.zeros((128, KX))
    spread = np.zeros((128, 256))
    for slot in range(64):
        part, block, column = slot // 32, slot % 32 // GY, slot % GY
        gather[slot, block, column, ROWS] = 1.0
        lane_part[slot, part * 128 : part * 128 + 128] = 1.0
        if block == 0:
            spread[slot, part * 128 : part * 128 + 128] = 1.0
        else:
            other = GX - block
            join[slot, part * 512 + other * 32] = 1.0 - 2.0 * part
    return (
        low(row_order.reshape(ROWS * M, MEMBERS * GY * PAD)),
        low(pick.reshape(ROWS * M, 256)),
        same.reshape(ROWS * M, 128).astype(np.float32),
        low(gather.reshape(128, DESTS // 2 * PAD)),
        lane_part.astype(np.float32),
        low(join),
        low(spread),
    )


def nn(a, b):
    return jnp.dot(a, b, preferred_element_type=jnp.float32)


def nt(a, b):
    return lax.dot_general(a, b, (((1,), (1,)), ((), ())), preferred_element_type=jnp.float32)


def place(block, rows):
    negative = (block < GX // 2).astype(jnp.int32)
    return negative, jnp.where(negative == 1, WAVES * (GX // 2 - 1 - block), WAVES * (block - GX // 2))


def pair_mask(base, negative, cut):
    shape = (2 * MEMBERS * HALF, KY)
    wave = base + HALF * negative + (lax.broadcasted_iota(jnp.int32, shape, 0) & (HALF - 1))
    wave_y = lax.broadcasted_iota(jnp.int32, shape, 1)
    return wave * wave + wave_y * wave_y < cut


def own_kernel(cut_ref, own_ref, fold_ref, coarse_ref, fine_ref, folded_ref, extra_ref, scale_ref):
    block = lax.axis_index("gx")
    cut = cut_ref[lax.axis_index("band")]
    negative, base = place(block, WAVES)
    fold = fold_ref[negative, :, : WAVES * MEMBERS]
    inside = pair_mask(base, negative, cut)
    for part in range(2):
        folded_ref[part] = jnp.where(inside, nn(fold, own_ref[part]), 0.0)

    wave_y = lax.broadcasted_iota(jnp.int32, (MEMBERS, KY), 1)
    last = base + WAVES
    edge = last * last + wave_y * wave_y < cut
    edge_real = jnp.where(edge, own_ref[0, :16].astype(jnp.float32)[:MEMBERS], 0.0)
    edge_imag = jnp.where(edge, own_ref[1, :16].astype(jnp.float32)[:MEMBERS], 0.0)
    cosine, sine = fine_ref[0], fine_ref[1]
    even = jnp.concatenate(
        [edge_real[m : m + 1] * cosine - edge_imag[m : m + 1] * sine for m in range(MEMBERS)], axis=0
    )
    odd = jnp.concatenate(
        [edge_real[m : m + 1] * sine + edge_imag[m : m + 1] * cosine for m in range(MEMBERS)], axis=0
    )
    turned = jnp.concatenate(
        [jnp.concatenate([even, -odd], axis=1), jnp.concatenate([odd, even], axis=1)], axis=0
    ).astype(jnp.bfloat16)
    extra_ref[...] = nt(coarse_ref[...], turned)

    shape = (KX, KY)
    wave_x = lax.broadcasted_iota(jnp.int32, shape, 0) - KX // 2
    wave_y = lax.broadcasted_iota(jnp.int32, shape, 1)
    inside = (wave_x * wave_x + wave_y * wave_y < cut).astype(jnp.float32)
    count = jnp.sum(jnp.sum(inside.reshape(KX // 8, 8, KY), axis=0))
    scale_ref[...] = lax.rsqrt(jnp.full((8, 128), count)) * (1.0 / math.sqrt(M * BANDS))


def rows_kernel(cut_ref, folded_ref, extra_ref, mirror_ref, fold_ref, table_ref, out_ref):
    cut = cut_ref[lax.axis_index("band")]
    negative, base = place(lax.axis_index("gx"), WAVES)
    fold = fold_ref[negative, :, WAVES * MEMBERS :]
    inside = pair_mask(base, negative, cut)
    real = folded_ref[0] + jnp.where(inside, nn(fold, mirror_ref[0]), 0.0)
    imag = folded_ref[1] + jnp.where(inside, nn(fold, mirror_ref[1]), 0.0)
    half = MEMBERS * HALF
    with_cosine = jnp.concatenate([real[:half], imag[half:]], axis=0)
    with_sine = jnp.concatenate([-imag[:half], real[half:]], axis=0)
    weights = jnp.concatenate([with_cosine, with_sine], axis=1).astype(jnp.bfloat16)
    dests = DESTS // 4
    row = lax.broadcasted_iota(jnp.int32, (dests, PAD, 256), 1)
    for part in range(4):
        rows = pl.ds(part * dests * PAD, dests * PAD)
        block = nt(table_ref[rows, :], weights).reshape(dests, PAD, 256)
        extra = extra_ref[part * dests : (part + 1) * dests, :].reshape(dests, 1, 256)
        out_ref[rows, :] = jnp.where(row == ROWS, extra, block).reshape(dests * PAD, 256).astype(jnp.bfloat16)


def weigh(alpha, edge, last_ref, start, ensemble_ref, chunk, scale_ref):
    columns = pl.ds(pl.multiple_of(start, CHUNK), CHUNK)
    repeat = CHUNK // 128
    cosine, sine = last_ref[:1, columns], last_ref[1:2, columns]
    alpha = alpha + jnp.concatenate([edge[:, :128]] * repeat, axis=1) * cosine
    alpha = alpha + jnp.concatenate([edge[:, 128:]] * repeat, axis=1) * sine
    fields = ensemble_ref[:, :, pl.ds(pl.multiple_of(chunk * CHUNK, CHUNK), CHUNK)].astype(jnp.float32)
    return jnp.sum(alpha.reshape(ROWS, M, CHUNK) * fields, axis=1) * scale_ref[:1, :1]


def far_kernel(
    scale_ref,
    got_ref,
    ensemble_ref,
    table_ref,
    row_ref,
    pick_ref,
    same_ref,
    gather_ref,
    part_ref,
    join_ref,
    spread_ref,
    last_ref,
    joined_ref,
    edge_ref,
    relay_ref,
):
    span = GY * PAD
    members = []
    for m in range(MEMBERS):
        pieces = []
        for part in range(2):
            lane = part * 128 + m * HALF
            pieces += [got_ref[block * span : (block + 1) * span, lane : lane + HALF] for block in range(GX)]
        members.append(jnp.concatenate(pieces, axis=1))
    edge = nn(
        gather_ref[...],
        got_ref[: GX // 2 * GY * PAD, :],
    )
    edge = (nt(pick_ref[...], (edge * part_ref[...]).astype(jnp.bfloat16)) * same_ref[...]).astype(jnp.bfloat16)
    joined = nn(
        jnp.concatenate([row_ref[...], edge], axis=1), jnp.concatenate(members + [join_ref[...]], axis=0)
    ).astype(jnp.bfloat16)
    joined_ref[...] = joined
    edge = nn(edge, spread_ref[...])
    edge_ref[...] = edge
    chunk = BANDS - 1 - (lax.axis_index("band") ^ 1)
    start = pl.multiple_of(chunk * CHUNK, CHUNK)
    alpha = nn(joined, table_ref[:, pl.ds(start, CHUNK)])
    relay_ref[...] = weigh(alpha, edge, last_ref, start, ensemble_ref, chunk, scale_ref).astype(relay_ref.dtype)


def chunk_field(chunk, joined, edge, last_ref, ensemble_ref, table_ref, scale_ref):
    start = pl.multiple_of(chunk * CHUNK, CHUNK)
    alpha = nn(joined, table_ref[:, pl.ds(start, CHUNK)])
    return weigh(alpha, edge, last_ref, start, ensemble_ref, chunk, scale_ref)


def near_kernel(scale_ref, joined_ref, edge_ref, ensemble_ref, table_ref, last_ref, direct_ref, mirrored_ref):
    band = lax.axis_index("band")
    refs = (last_ref, ensemble_ref, table_ref, scale_ref)
    joined, edge = joined_ref[...], edge_ref[...]
    mirrored_ref[...] = chunk_field(BANDS - 1 - band, joined, edge, *refs)
    direct_ref[...] = chunk_field(band ^ 1, joined, edge, *refs).astype(direct_ref.dtype)


def own_field_kernel(scale_ref, joined_ref, edge_ref, ensemble_ref, table_ref, last_ref, own_ref):
    band = lax.axis_index("band")
    own_ref[...] = chunk_field(
        band, joined_ref[...], edge_ref[...], last_ref, ensemble_ref, table_ref, scale_ref
    )


def whole(count):
    return [pl.BlockSpec(memory_space=pltpu.VMEM) for _ in range(count)]


def body(ensemble, spectral, band_cut):
    own = spectral[0].reshape(2, WAVES * MEMBERS, KY)
    mirror = lax.ppermute(spectral[0, :, HALF:], "gx", [(i, GX - 1 - i) for i in range(GX)])
    mirror = mirror.reshape(2, HALF * MEMBERS, KY)
    table_y, coarse, fine = row_tables()
    smem = pl.BlockSpec(memory_space=pltpu.SMEM)
    folded, extra, scale = pl.pallas_call(
        own_kernel,
        out_shape=[
            jax.ShapeDtypeStruct((2, 256, KY), jnp.float32),
            jax.ShapeDtypeStruct((DESTS, 256), jnp.float32),
            jax.ShapeDtypeStruct((8, 128), jnp.float32),
        ],
        in_specs=[smem] + whole(4),
        out_specs=whole(3),
        compiler_params=pltpu.CompilerParams(vmem_limit_bytes=SCRATCH),
        cost_estimate=pl.CostEstimate(flops=OWN_FLOPS, bytes_accessed=1 << 20, transcendentals=0),
        name="own_kernel",
    )(band_cut, own, fold_tables(), coarse, fine)
    rows = pl.pallas_call(
        rows_kernel,
        out_shape=jax.ShapeDtypeStruct((DESTS * PAD, 256), jnp.bfloat16),
        in_specs=[smem] + whole(5),
        out_specs=pl.BlockSpec(memory_space=pltpu.VMEM),
        compiler_params=pltpu.CompilerParams(vmem_limit_bytes=SCRATCH),
        cost_estimate=pl.CostEstimate(flops=ROWS_FLOPS, bytes_accessed=4 << 20, transcendentals=0),
        name="rows_kernel",
    )(band_cut, folded, extra, mirror, fold_tables(), table_y)
    got = lax.all_to_all(rows, ("gx", "gy"), split_axis=0, concat_axis=0, tiled=True)
    fields, (table_x, last) = ensemble[0].transpose(1, 0, 2), column_tables()
    piece = jax.ShapeDtypeStruct((ROWS, CHUNK), jnp.float32)
    sent = jax.ShapeDtypeStruct((ROWS, CHUNK), SENT)
    joined, edge, relay = pl.pallas_call(
        far_kernel,
        out_shape=[
            jax.ShapeDtypeStruct((ROWS * M, KX), jnp.bfloat16),
            jax.ShapeDtypeStruct((ROWS * M, 256), jnp.float32),
            sent,
        ],
        in_specs=whole(12),
        out_specs=whole(3),
        compiler_params=pltpu.CompilerParams(vmem_limit_bytes=SCRATCH),
        cost_estimate=pl.CostEstimate(flops=3 << 30, bytes_accessed=8 << 20, transcendentals=0),
        name="far_kernel",
    )(scale, got, fields, table_x, *order_tables(), last)
    relay = ahead(relay, 1)
    direct, mirrored = pl.pallas_call(
        near_kernel,
        out_shape=[sent, piece],
        in_specs=whole(6),
        out_specs=whole(2),
        compiler_params=pltpu.CompilerParams(vmem_limit_bytes=SCRATCH),
        cost_estimate=pl.CostEstimate(flops=NEAR_FLOPS, bytes_accessed=4 << 20, transcendentals=0),
        name="near_kernel",
    )(scale, joined, edge, fields, table_x, last)
    direct = ahead(direct, 1)
    passed = (mirrored + relay.astype(jnp.float32)).astype(SENT)
    passed, joined = lax.optimization_barrier((passed, joined))
    across = ahead(passed, 3)
    own = pl.pallas_call(
        own_field_kernel,
        out_shape=piece,
        in_specs=whole(6),
        out_specs=pl.BlockSpec(memory_space=pltpu.VMEM),
        compiler_params=pltpu.CompilerParams(vmem_limit_bytes=SCRATCH),
        cost_estimate=pl.CostEstimate(flops=NEAR_FLOPS, bytes_accessed=4 << 20, transcendentals=0),
        name="own_field_kernel",
    )(scale, joined, edge, fields, table_x, last)
    return (own + direct.astype(jnp.float32)) + across.astype(jnp.float32)


def ahead(piece, step):
    return lax.ppermute(piece, "band", [(i, i ^ step) for i in range(BANDS)])


def solution(mesh):
    placed = (P("band", None, ("gx", "gy"), None), P("band", None, "gx", "gy", None), P())
    return jax.shard_map(
        body, mesh=mesh, in_specs=placed, out_specs=P(("gx", "gy"), "band"), check_vma=False
    )
```
